128 devices in a mesh: band: 8 (over x, y_hi), grow: 16 (over y_lo, z, core).
Axes of the slice: x: 4, y: 4 (y_hi: 2, y_lo: 2; y = y_hi * 2 + y_lo), z: 4, core: 2. Of those that a mesh axis runs over, the one named last changes fastest.
Arguments:
- chi_prev: float32 [15360, 4096], P('band', 'grow'), may hold values from -6 to 6
- zeta_rows: bfloat16 [15360, 8192], P(('band', 'grow')), may hold values from -0.0625 to 0.0625
- zeta_slab: bfloat16 [4096, 8192], P('grow'), may hold values from -0.0625 to 0.0625
- valence_store: bfloat16 [8, 128, 8192], P('band'), may hold values from -6 to 6
- valence_energy: float32 [8, 128], replicated, may hold values from -6 to -0.5
- conduction: bfloat16 [16, 8192], P('grow'), may hold values from -6 to 6
- conduction_energy: float32 [16], replicated, may hold values from 0.5 to 8
- owners: int32 [2], replicated, may hold values from 0 to 7, as said below
- gmap_rows: int32 [15360], P(('band', 'grow')), may hold values from 0 to 262143
- gmap_slab: int32 [4096], P('grow'), may hold values from 0 to 262143
Outputs:
- chi_new: float32 [15360, 4096], P('band', 'grow')
The draws below stay inside these ranges and needn't reach their ends.
Inputs may be any that keep to these rules, and one draw needn't show every extreme that they name: `owners`: 2 different indices of stored panels; the last stored panel is always one of them, at a varying place.
All inputs are finite; a program needn't handle non-finite values.
Results may differ from the reference program's by a relative error of at most 0.0039.
Values may be sent and summed in bfloat16 or wider, within the bound.
No kernel may reach another device: no remote copies, remote signals or barrier semaphores. Data moves between devices by JAX's collectives and lax.ppermute only.
A program may use at most 256 MiB of HBM per device.

```python
import math
import jax
import jax.numpy as jnp
from jax import lax

NG = 15360
NGS = 4096
NMU = 8192
BOX = 64
PANEL = 128
NPAN = 2
NC = 16
OWNERS = 8


def draw_owners(key, part):
    key = jax.random.fold_in(key, 7)
    key_order, key_slot = jax.random.split(key)
    others = jax.random.permutation(key_order, OWNERS - 1)[:NPAN - 1]
    chosen = jnp.concatenate([others.astype(jnp.int32), jnp.full((1,), OWNERS - 1, jnp.int32)])
    offset = jax.random.randint(key_slot, (), 0, NPAN)
    return jnp.roll(chosen, offset).astype(jnp.int32)


def plant(values, stream_key, smallest, top_value):
    shape = values.shape
    index_at = [jax.random.randint(jax.random.fold_in(stream_key, axis), (), 0, shape[axis]) for axis in range(len(shape))]
    values = values.at[tuple(index_at)].set(smallest)
    longest = shape.index(max(shape))
    index_at[longest] = (index_at[longest] + 1) % shape[longest]
    return values.at[tuple(index_at)].set(top_value)


def shard_levels(key, shape, pieces, low, largest):
    level = 1.0
    for position, blocks in pieces:
        heights = jax.random.uniform(jax.random.fold_in(jax.random.fold_in(key, 6), position), (blocks,), jnp.float32, low / len(pieces), largest / len(pieces))
        level = level * jnp.repeat(jnp.exp(heights), shape[position] // blocks).reshape((-1,) + (1,) * (len(shape) - 1 - position))
    return level


def bell_draw(stream_key, shape, spread, most, cuts=(), held_as=jnp.bfloat16):
    drawn = spread * jax.random.normal(stream_key, shape, jnp.float32)
    if cuts:
        drawn = drawn * shard_levels(stream_key, shape, cuts, -0.22, 0.18)
    return jnp.clip(drawn, -most, most).astype(held_as)


def setup_inputs(seed: int = 0) -> dict:
    keys = jax.random.split(jax.random.key(seed), 11)
    return {
        "chi_prev": bell_draw(keys[0], (NG, NGS), 1.0, 6.0, ((0, 8), (1, 16)), jnp.float32),
        "zeta_rows": bell_draw(keys[1], (NG, NMU), NMU ** -0.5, 0.0625, ((0, 128),)),
        "zeta_slab": bell_draw(keys[2], (NGS, NMU), NMU ** -0.5, 0.0625, ((0, 16),)),
        "valence_store": bell_draw(keys[3], (OWNERS, PANEL, NMU), 1.0, 6.0, ((0, 8),)),
        "valence_energy": jnp.clip(jax.random.uniform(keys[4], (OWNERS, PANEL), jnp.float32, -6.0, -0.5), -6.0, -0.5),
        "conduction": bell_draw(keys[5], (NC, NMU), 1.0, 6.0, ((0, 16),)),
        "conduction_energy": jnp.clip(jax.random.uniform(keys[6], (NC,), jnp.float32, 0.5, 8.0), 0.5, 8.0),
        "owners": draw_owners(jax.random.fold_in(keys[10], 71), 0),
        "gmap_rows": plant(jax.random.randint(keys[8], (NG,), 0, BOX ** 3), jax.random.fold_in(keys[8], 1), 0, (BOX ** 3) - 1).astype(jnp.int32),
        "gmap_slab": plant(jax.random.randint(keys[9], (NGS,), 0, BOX ** 3), jax.random.fold_in(keys[9], 1), 0, (BOX ** 3) - 1).astype(jnp.int32),
    }


def coulomb_root(box_index):
    plane_size = BOX * BOX
    half_box = BOX // 2
    leading = box_index // plane_size
    middle = box_index // BOX % BOX
    trailing = box_index % BOX

    def centred(offset_idx):
        return jnp.where(offset_idx >= half_box, offset_idx - BOX, offset_idx).astype(jnp.float32)
    length_sq = centred(leading) ** 2 + centred(middle) ** 2 + centred(trailing) ** 2
    return 32.0 / jnp.sqrt(length_sq + 64.0)

def contract_last(left, right):
    return lax.dot_general(left, right, (((1,), (1,)), ((), ())), preferred_element_type=jnp.float32)

def reference(chi_prev, zeta_rows, zeta_slab, valence_store, valence_energy, conduction, conduction_energy, owners, gmap_rows, gmap_slab):
    valence = jnp.take(valence_store, owners, axis=0).reshape(NPAN * PANEL, NMU)
    val_energy = jnp.take(valence_energy, owners, axis=0).reshape(-1)
    norm_factor = 4.0 / math.sqrt(NPAN * PANEL * NC)
    weights = norm_factor / (conduction_energy[None, :] - val_energy[:, None])
    root_rows = coulomb_root(gmap_rows)
    root_slab = coulomb_root(gmap_slab)
    val_wide = valence.astype(jnp.float32)
    total = jnp.zeros((NG, NGS), jnp.float32)
    for cond_idx in range(NC):
        pair = (val_wide * conduction[cond_idx].astype(jnp.float32)[None, :]).astype(jnp.bfloat16)
        rho = (root_rows[:, None] * contract_last(zeta_rows, pair)).astype(jnp.bfloat16)
        slab = (root_slab[:, None] * contract_last(zeta_slab, pair) * weights[:, cond_idx][None, :]).astype(jnp.bfloat16)
        total = total + contract_last(rho, slab)
    return chi_prev - total
```

```python
import math

import jax
import jax.numpy as jnp
from jax import lax
from jax.experimental import pallas as pl
from jax.experimental.pallas import tpu as pltpu
from jax.sharding import PartitionSpec as P

BOX = 64
KC = 1024
VMEM = 56 * 1024 * 1024
BF = jnp.bfloat16
F32 = jnp.float32


def coulomb_root(box_index):
    plane_size = BOX * BOX
    half_box = BOX // 2
    leading = box_index // plane_size
    middle = box_index // BOX % BOX
    trailing = box_index % BOX

    def centred(offset_idx):
        return jnp.where(offset_idx >= half_box, offset_idx - BOX, offset_idx).astype(F32)

    length_sq = centred(leading) ** 2 + centred(middle) ** 2 + centred(trailing) ** 2
    return 32.0 / jnp.sqrt(length_sq + 64.0)


def linear(x, y, z, core):
    return ((x * 2 + y // 2) * 16) + (y % 2) * 8 + z * 2 + core


def route(step):
    pairs = []
    for x in range(4):
        for y in range(4):
            for z in range(4):
                for core in range(2):
                    pairs.append((linear(x, y, z, core), linear(*step(x, y, z, core))))
    return pairs


Z_UP = route(lambda x, y, z, c: (x, y, (z + 1) % 4, c))
Z_DOWN = route(lambda x, y, z, c: (x, y, (z + 3) % 4, c))
CORE = route(lambda x, y, z, c: (x, y, z, 1 - c))
X_PAIR = route(lambda x, y, z, c: (x ^ 1, y, z, c))
Y_PAIR = route(lambda x, y, z, c: (x, y ^ 1, z, c))
Y_CROSS = route(lambda x, y, z, c: (x, 3 - y, z, c))


def send(value, pairs):
    return lax.ppermute(value, ("band", "grow"), pairs)


def nt_dot(left, right):
    return lax.dot_general(left, right, (((1,), (1,)), ((), ())), preferred_element_type=F32)


def slab_body(val, cond, zeta, weight, root, out, lhs, acc):
    step = pl.program_id(0)
    conds = cond.shape[0]
    for c in range(conds):
        lhs[c * 128 : (c + 1) * 128, :] = val[...] * cond[c : c + 1, :]
    part = nt_dot(lhs[...], zeta[...])

    @pl.when(step == 0)
    def _():
        acc[...] = part

    @pl.when(step > 0)
    def _():
        acc[...] += part

    @pl.when(step == pl.num_programs(0) - 1)
    def _():
        out[...] = (acc[...] * root[...] * weight[...]).astype(BF)


def slab_kernel(val, cond, zeta, weight, root):
    conds, points = cond.shape
    pairs = conds * 128
    cols = zeta.shape[0]
    return pl.pallas_call(
        slab_body,
        grid=(points // KC,),
        in_specs=[
            pl.BlockSpec((128, KC), lambda k: (0, k)),
            pl.BlockSpec((conds, KC), lambda k: (0, k)),
            pl.BlockSpec((cols, KC), lambda k: (0, k)),
            pl.BlockSpec((pairs, 1), lambda k: (0, 0)),
            pl.BlockSpec((1, cols), lambda k: (0, 0)),
        ],
        out_specs=pl.BlockSpec((pairs, cols), lambda k: (0, 0)),
        out_shape=jax.ShapeDtypeStruct((pairs, cols), BF),
        scratch_shapes=[pltpu.VMEM((pairs, KC), BF), pltpu.VMEM((pairs, cols), F32)],
        compiler_params=pltpu.CompilerParams(vmem_limit_bytes=VMEM),
        cost_estimate=pl.CostEstimate(
            flops=2 * pairs * cols * points, bytes_accessed=8 << 20, transcendentals=0
        ),
        name="slab_pairs",
    )(val, cond, zeta, weight, root)


def rho_body(zeta, cond, val_a, val_b, root, out, lhs, rhs, acc):
    step = pl.program_id(0)
    conds = cond.shape[0]
    rows = zeta.shape[0]

    @pl.when(step == 0)
    def _():
        lhs[...] = jnp.zeros_like(lhs)

    for c in range(conds):
        lhs[c * 128 : c * 128 + rows, :] = zeta[...] * cond[c : c + 1, :]
    rhs[0:128, :] = val_a[...]
    rhs[128:256, :] = val_b[...]
    part = nt_dot(lhs[...], rhs[...])

    @pl.when(step == 0)
    def _():
        acc[...] = part

    @pl.when(step > 0)
    def _():
        acc[...] += part

    @pl.when(step == pl.num_programs(0) - 1)
    def _():
        for c in range(conds):
            block = acc[c * 128 : c * 128 + rows, :] * root[...]
            out[0, :, c * 128 : (c + 1) * 128] = block[:, 0:128].astype(BF)
            out[1, :, c * 128 : (c + 1) * 128] = block[:, 128:256].astype(BF)


def rho_kernel(zeta, cond, val_a, val_b, root):
    conds, points = cond.shape
    rows = zeta.shape[0]
    return pl.pallas_call(
        rho_body,
        grid=(points // KC,),
        in_specs=[
            pl.BlockSpec((rows, KC), lambda k: (0, k)),
            pl.BlockSpec((conds, KC), lambda k: (0, k)),
            pl.BlockSpec((128, KC), lambda k: (0, k)),
            pl.BlockSpec((128, KC), lambda k: (0, k)),
            pl.BlockSpec((rows, 1), lambda k: (0, 0)),
        ],
        out_specs=pl.BlockSpec((2, rows, conds * 128), lambda k: (0, 0, 0)),
        out_shape=jax.ShapeDtypeStruct((2, rows, conds * 128), BF),
        scratch_shapes=[
            pltpu.VMEM((conds * 128, KC), BF),
            pltpu.VMEM((256, KC), BF),
            pltpu.VMEM((conds * 128, 256), F32),
        ],
        compiler_params=pltpu.CompilerParams(vmem_limit_bytes=VMEM),
        cost_estimate=pl.CostEstimate(
            flops=2 * conds * 128 * 256 * points, bytes_accessed=8 << 20, transcendentals=0
        ),
        name="rho_rows",
    )(zeta, cond, val_a, val_b, root)


def chi_kernel(parts, slab_a, slab_b, out_dtype, name):
    _, rows, depth = parts[0][0].shape
    cols = slab_a.shape[1]
    count = len(parts)
    blk = 1024

    def body(*refs):
        ins = refs[:count]
        slab_0, slab_1, out, lhs, acc = refs[count:]
        step = pl.program_id(0)

        @pl.when(step == 0)
        def _():
            lhs[...] = jnp.zeros_like(lhs)
            acc[...] = jnp.zeros_like(acc)

        total = acc[...]
        for half, slab in ((0, slab_0), (1, slab_1)):
            for i in range(count):
                which = 1 - half if parts[i][1] else half
                lhs[half, i * 128 : i * 128 + rows, :] = ins[i][which]
            total += jnp.dot(lhs[half], slab[...], preferred_element_type=F32)
        acc[...] = total

        @pl.when(step == pl.num_programs(0) - 1)
        def _():
            for i in range(count):
                out[i] = acc[i * 128 : i * 128 + rows, :].astype(out_dtype)

    return pl.pallas_call(
        body,
        grid=(depth // blk,),
        in_specs=[pl.BlockSpec((2, rows, blk), lambda k: (0, 0, k))] * count
        + [pl.BlockSpec((blk, cols), lambda k: (k, 0))] * 2,
        out_specs=pl.BlockSpec((count, rows, cols), lambda k: (0, 0, 0)),
        out_shape=jax.ShapeDtypeStruct((count, rows, cols), out_dtype),
        scratch_shapes=[
            pltpu.VMEM((2, count * 128, blk), BF),
            pltpu.VMEM((count * 128, cols), F32),
        ],
        compiler_params=pltpu.CompilerParams(vmem_limit_bytes=VMEM),
        cost_estimate=pl.CostEstimate(
            flops=2 * count * rows * cols * 2 * depth,
            bytes_accessed=count * rows * depth * 4 + depth * cols * 4,
            transcendentals=0,
        ),
        name=name,
    )(*[p[0] for p in parts], slab_a, slab_b)


def finish_kernel(place, chi, mine_a, mine_b, theirs_a, theirs_b):
    total_rows, cols = chi.shape
    rows = mine_a.shape[1]
    chi_blocks = chi.reshape(total_rows // rows, rows, cols)

    def body(place_ref, chi_ref, ma, mb, ta, tb, out):
        step = pl.program_id(0)
        core = place_ref[8]
        for first, src in ((0, ma), (3, mb), (4, ta), (7, tb)):
            last = {0: 3, 3: 4, 4: 7, 7: 8}[first]

            @pl.when(jnp.logical_and(step >= first, step < last))
            def _(src=src):
                out[core] = chi_ref[core] - src[0].astype(F32)
                out[1 - core] = chi_ref[1 - core] - src[1].astype(F32)

    def slot(first, count):
        return lambda i, place_ref: (jnp.clip(i - first, 0, count - 1), 0, 0)

    where = lambda i, place_ref: (place_ref[i], 0, 0)
    grid_spec = pltpu.PrefetchScalarGridSpec(
        num_scalar_prefetch=1,
        grid=(8,),
        in_specs=[
            pl.BlockSpec((2, rows, cols), where),
            pl.BlockSpec((2, rows, cols), slot(0, 3)),
            pl.BlockSpec((2, rows, cols), slot(3, 1)),
            pl.BlockSpec((2, rows, cols), slot(4, 3)),
            pl.BlockSpec((2, rows, cols), slot(7, 1)),
        ],
        out_specs=pl.BlockSpec((2, rows, cols), where),
    )
    return pl.pallas_call(
        body,
        grid_spec=grid_spec,
        out_shape=jax.ShapeDtypeStruct(chi_blocks.shape, F32),
        compiler_params=pltpu.CompilerParams(vmem_limit_bytes=VMEM),
        cost_estimate=pl.CostEstimate(flops=0, bytes_accessed=6 << 20, transcendentals=0),
        name="finish",
    )(place, chi_blocks, mine_a, mine_b, theirs_a, theirs_b).reshape(total_rows, cols)


def on_device(
    chi_prev,
    zeta_rows,
    zeta_slab,
    valence_store,
    valence_energy,
    conduction,
    conduction_energy,
    owners,
    gmap_rows,
    gmap_slab,
):
    band = lax.axis_index("band")
    grow = lax.axis_index("grow")
    core = grow % 2
    yz = grow // 2
    turn = (band // 2 + band % 2) % 2
    points = valence_store.shape[2]

    store = valence_store[0]
    piece_a = lax.dynamic_slice_in_dim(store, yz * 16 + core * 8, 8, 0)
    piece_b = lax.dynamic_slice_in_dim(store, yz * 16 + (1 - core) * 8, 8, 0)
    turns = [(b // 2 + b % 2) % 2 for b in range(8)]
    pieces = jnp.stack([piece_b if t else piece_a for t in turns])
    panels = lax.all_to_all(pieces, "band", split_axis=0, concat_axis=0, tiled=True)
    chosen = jnp.concatenate(
        [lax.dynamic_slice_in_dim(panels, owners[i], 1, 0)[0] for i in range(2)], axis=0
    )
    payload = jnp.concatenate([chosen, conduction.reshape(16, points // 16)], axis=1)
    width = payload.shape[1]
    groups = [list(range(0, 16, 2)), list(range(1, 16, 2))]
    mine = lax.all_to_all(
        jnp.broadcast_to(payload[None], (8, 16, width)),
        "grow",
        split_axis=0,
        concat_axis=0,
        tiled=True,
        axis_index_groups=groups,
    ).reshape(128, width)
    other = send(mine, CORE)

    cond_mine = mine[:, points:].reshape(8, points)
    cond_other = other[:, points:].reshape(8, points)
    cond = jnp.concatenate(
        [
            jnp.where(core == 0, cond_mine, cond_other),
            jnp.where(core == 0, cond_other, cond_mine),
        ],
        axis=0,
    )
    energy_c = conduction_energy.reshape(8, 2).T.reshape(16)
    energy_v = jnp.take(valence_energy, owners, axis=0).reshape(2, 8, 2, 8)
    half = (core + turn) % 2
    energy_v = lax.dynamic_index_in_dim(energy_v, half, 2, keepdims=False)
    energy_v = energy_v.transpose(1, 0, 2).reshape(128)
    weight = (4.0 / math.sqrt(4096)) / (energy_c[:, None] - energy_v[None, :])

    rho = rho_kernel(zeta_rows, cond, mine, other, coulomb_root(gmap_rows)[:, None])
    slab_pp = slab_kernel(
        mine, cond, zeta_slab, weight.reshape(2048, 1), coulomb_root(gmap_slab)[None, :]
    )

    from_down = send(rho, Z_UP)
    from_up = send(rho, Z_DOWN)
    rho_x = send(rho, CORE)
    slab_px = send(slab_pp, X_PAIR)
    slab_yp = send(slab_pp, Y_PAIR)
    slab_yx = send(slab_pp, Y_CROSS)
    far_0 = send(from_down[0], Z_UP)
    far_1 = send(from_up[1], Z_DOWN)
    from_down_x = send(from_down, CORE)
    from_up_x = send(from_up, CORE)
    far = jnp.stack([far_0, far_1])
    far_x = send(far, CORE)

    near = [
        (rho, False),
        (rho_x, True),
        (from_down, False),
        (from_down_x, True),
        (from_up, False),
        (from_up_x, True),
    ]
    rest = [(far, False), (far_x, True)]
    near_out = chi_kernel(near, slab_yp, slab_yx, BF, "chi_near_out")
    near_in = chi_kernel(near, slab_pp, slab_px, F32, "chi_near_in")
    got_near = send(near_out, Y_PAIR)
    rest_out = chi_kernel(rest, slab_yp, slab_yx, BF, "chi_far_out")
    got_rest = send(rest_out, Y_PAIR)
    rest_in = chi_kernel(rest, slab_pp, slab_px, F32, "chi_far_in")

    yl = grow // 8
    z = yz % 4
    slots = jnp.stack([z, (z + 3) % 4, (z + 1) % 4, (z + 2) % 4]).astype(jnp.int32)
    place = jnp.concatenate([yl * 4 + slots, (1 - yl) * 4 + slots, core[None]]).astype(jnp.int32)
    return finish_kernel(place, chi_prev, near_in, rest_in, got_near, got_rest)


def solution(mesh):
    placed = (
        P("band", "grow"),
        P(("band", "grow"), None),
        P("grow", None),
        P("band", None, None),
        P(),
        P("grow", None),
        P(),
        P(),
        P(("band", "grow")),
        P("grow"),
    )
    return jax.shard_map(
        on_device, mesh=mesh, in_specs=placed, out_specs=P("band", "grow"), check_vma=False
    )
```

```python
import math

import jax
import jax.numpy as jnp
from jax import lax
from jax.experimental import pallas as pl
from jax.experimental.pallas import tpu as pltpu
from jax.sharding import PartitionSpec as P

BOX = 64
KC = 2048
VMEM = 56 * 1024 * 1024
BF = jnp.bfloat16
F32 = jnp.float32


def coulomb_root(box_index):
    plane_size = BOX * BOX
    half_box = BOX // 2
    leading = box_index // plane_size
    middle = box_index // BOX % BOX
    trailing = box_index % BOX

    def centred(offset_idx):
        return jnp.where(offset_idx >= half_box, offset_idx - BOX, offset_idx).astype(F32)

    length_sq = centred(leading) ** 2 + centred(middle) ** 2 + centred(trailing) ** 2
    return 32.0 / jnp.sqrt(length_sq + 64.0)


def linear(x, y, z, core):
    return ((x * 2 + y // 2) * 16) + (y % 2) * 8 + z * 2 + core


def route(step):
    pairs = []
    for x in range(4):
        for y in range(4):
            for z in range(4):
                for core in range(2):
                    pairs.append((linear(x, y, z, core), linear(*step(x, y, z, core))))
    return pairs


Z_UP = route(lambda x, y, z, c: (x, y, (z + 1) % 4, c))
Z_DOWN = route(lambda x, y, z, c: (x, y, (z + 3) % 4, c))
CORE = route(lambda x, y, z, c: (x, y, z, 1 - c))
X_PAIR = route(lambda x, y, z, c: (x ^ 1, y, z, c))
Y_PAIR = route(lambda x, y, z, c: (x, y ^ 1, z, c))
Y_CROSS = route(lambda x, y, z, c: (x, 3 - y, z, c))


def send(value, pairs):
    return lax.ppermute(value, ("band", "grow"), pairs)


def nt_dot(left, right):
    return lax.dot_general(left, right, (((1,), (1,)), ((), ())), preferred_element_type=F32)


def slab_body(val, cond, zeta, weight, root, out, acc):
    step = pl.program_id(0)
    conds = cond.shape[0]
    for c in range(0, conds, 4):
        lhs = jnp.concatenate([val[...] * cond[c + i : c + i + 1, :] for i in range(4)], axis=0)
        part = nt_dot(lhs, zeta[...])
        rows = slice(c * 128, (c + 4) * 128)
        acc[rows] = jnp.where(step == 0, part, acc[rows] + part)

    @pl.when(step == pl.num_programs(0) - 1)
    def _():
        out[...] = (acc[...] * root[...] * weight[...]).astype(BF)


def slab_kernel(val, cond, zeta, weight, root):
    conds, points = cond.shape
    pairs = conds * 128
    cols = zeta.shape[0]
    return pl.pallas_call(
        slab_body,
        grid=(points // KC,),
        in_specs=[
            pl.BlockSpec((128, KC), lambda k: (0, k)),
            pl.BlockSpec((conds, KC), lambda k: (0, k)),
            pl.BlockSpec((cols, KC), lambda k: (0, k)),
            pl.BlockSpec((pairs, 1), lambda k: (0, 0)),
            pl.BlockSpec((1, cols), lambda k: (0, 0)),
        ],
        out_specs=pl.BlockSpec((pairs, cols), lambda k: (0, 0)),
        out_shape=jax.ShapeDtypeStruct((pairs, cols), BF),
        scratch_shapes=[pltpu.VMEM((pairs, cols), F32)],
        compiler_params=pltpu.CompilerParams(vmem_limit_bytes=VMEM),
        cost_estimate=pl.CostEstimate(
            flops=2 * pairs * cols * points, bytes_accessed=8 << 20, transcendentals=0
        ),
        name="slab_pairs",
    )(val, cond, zeta, weight, root)


def rho_body(zeta, cond, val_a, val_b, root, out, lhs, rhs, acc):
    step = pl.program_id(0)
    conds = cond.shape[0]
    rows = zeta.shape[0]

    @pl.when(step == 0)
    def _():
        lhs[...] = jnp.zeros_like(lhs)

    rhs[0:128, :] = val_a[...]
    rhs[128:256, :] = val_b[...]
    lhs[0:rows, :] = zeta[...]
    for c in range(0, conds, 4):
        left = jnp.concatenate([lhs[...] * cond[c + i : c + i + 1, :] for i in range(4)], axis=0)
        part = nt_dot(left, rhs[...])
        span = slice(c * 128, (c + 4) * 128)
        acc[span] = jnp.where(step == 0, part, acc[span] + part)

    @pl.when(step == pl.num_programs(0) - 1)
    def _():
        for c in range(conds):
            block = acc[c * 128 : c * 128 + rows, :] * root[...]
            out[0, :, c * 128 : (c + 1) * 128] = block[:, 0:128].astype(BF)
            out[1, :, c * 128 : (c + 1) * 128] = block[:, 128:256].astype(BF)


def rho_kernel(zeta, cond, val_a, val_b, root):
    conds, points = cond.shape
    rows = zeta.shape[0]
    return pl.pallas_call(
        rho_body,
        grid=(points // KC,),
        in_specs=[
            pl.BlockSpec((rows, KC), lambda k: (0, k)),
            pl.BlockSpec((conds, KC), lambda k: (0, k)),
            pl.BlockSpec((128, KC), lambda k: (0, k)),
            pl.BlockSpec((128, KC), lambda k: (0, k)),
            pl.BlockSpec((rows, 1), lambda k: (0, 0)),
        ],
        out_specs=pl.BlockSpec((2, rows, conds * 128), lambda k: (0, 0, 0)),
        out_shape=jax.ShapeDtypeStruct((2, rows, conds * 128), BF),
        scratch_shapes=[
            pltpu.VMEM((128, KC), BF),
            pltpu.VMEM((256, KC), BF),
            pltpu.VMEM((conds * 128, 256), F32),
        ],
        compiler_params=pltpu.CompilerParams(vmem_limit_bytes=VMEM),
        cost_estimate=pl.CostEstimate(
            flops=2 * conds * 128 * 256 * points, bytes_accessed=8 << 20, transcendentals=0
        ),
        name="rho_rows",
    )(zeta, cond, val_a, val_b, root)


def chi_kernel(arrays, parts, slab_a, slab_b, out_dtype, name):
    rows, depth = arrays[0].shape[-2:]
    cols = slab_a.shape[1]
    given, count = len(arrays), len(parts)
    blk = 1024

    def body(*refs):
        ins = refs[:given]
        slab_0, slab_1, out, lhs, acc = refs[given:]
        step = pl.program_id(0)

        @pl.when(step == 0)
        def _():
            lhs[...] = jnp.zeros_like(lhs)
            acc[...] = jnp.zeros_like(acc)

        total = acc[...]
        for half, slab in ((0, slab_0), (1, slab_1)):
            for i in range(count):
                array, index = parts[i][half]
                block = ins[array][...] if index is None else ins[array][index]
                lhs[half, i * 128 : i * 128 + rows, :] = block
            total += jnp.dot(lhs[half], slab[...], preferred_element_type=F32)
        acc[...] = total

        @pl.when(step == pl.num_programs(0) - 1)
        def _():
            for i in range(count):
                out[i] = acc[i * 128 : i * 128 + rows, :].astype(out_dtype)

    def spec(array):
        if array.ndim == 3:
            return pl.BlockSpec((2, rows, blk), lambda k: (0, 0, k))
        return pl.BlockSpec((rows, blk), lambda k: (0, k))

    return pl.pallas_call(
        body,
        grid=(depth // blk,),
        in_specs=[spec(a) for a in arrays] + [pl.BlockSpec((blk, cols), lambda k: (k, 0))] * 2,
        out_specs=pl.BlockSpec((count, rows, cols), lambda k: (0, 0, 0)),
        out_shape=jax.ShapeDtypeStruct((count, rows, cols), out_dtype),
        scratch_shapes=[
            pltpu.VMEM((2, count * 128, blk), BF),
            pltpu.VMEM((count * 128, cols), F32),
        ],
        compiler_params=pltpu.CompilerParams(vmem_limit_bytes=VMEM),
        cost_estimate=pl.CostEstimate(
            flops=2 * count * rows * cols * 2 * depth,
            bytes_accessed=count * rows * depth * 4 + depth * cols * 4,
            transcendentals=0,
        ),
        name=name,
    )(*arrays, slab_a, slab_b)


def finish_kernel(place, chi, mine, theirs, before, name):
    blocks, rows, cols = chi.shape
    count = mine.shape[0] // 2

    def body(place_ref, chi_ref, mine_ref, theirs_ref, *rest):
        out = rest[-1]
        step = pl.program_id(0)
        core = place_ref[2 * count]
        for first, src in ((0, mine_ref), (count, theirs_ref)):

            @pl.when(jnp.logical_and(step >= first, step < first + count))
            def _(src=src):
                out[core] = chi_ref[core] - src[0].astype(F32)
                out[1 - core] = chi_ref[1 - core] - src[1].astype(F32)

    def where(i, place_ref):
        return (place_ref[i], 0, 0)

    block = (2, rows, cols)
    specs = [
        pl.BlockSpec(block, where),
        pl.BlockSpec(block, lambda i, place_ref: (jnp.minimum(i, count - 1), 0, 0)),
        pl.BlockSpec(block, lambda i, place_ref: (jnp.maximum(i - count, 0), 0, 0)),
    ]
    operands = [place, chi, mine, theirs]
    if before is not None:
        specs.append(pl.BlockSpec(memory_space=pl.ANY))
        operands.append(before)
    return pl.pallas_call(
        body,
        grid_spec=pltpu.PrefetchScalarGridSpec(
            num_scalar_prefetch=1,
            grid=(2 * count,),
            in_specs=specs,
            out_specs=pl.BlockSpec(block, where),
        ),
        out_shape=jax.ShapeDtypeStruct(chi.shape, F32),
        input_output_aliases={} if before is None else {4: 0},
        compiler_params=pltpu.CompilerParams(vmem_limit_bytes=VMEM),
        cost_estimate=pl.CostEstimate(flops=0, bytes_accessed=count << 20, transcendentals=0),
        name=name,
    )(*operands)


def on_device(
    chi_prev,
    zeta_rows,
    zeta_slab,
    valence_store,
    valence_energy,
    conduction,
    conduction_energy,
    owners,
    gmap_rows,
    gmap_slab,
):
    band = lax.axis_index("band")
    grow = lax.axis_index("grow")
    core = grow % 2
    yz = grow // 2
    turn = (band // 2 + band % 2) % 2
    points = valence_store.shape[2]

    groups = [list(range(0, 16, 2)), list(range(1, 16, 2))]

    def over_plane(value):
        copies = jnp.broadcast_to(value[None], (8,) + value.shape)
        return lax.all_to_all(
            copies, "grow", split_axis=0, concat_axis=0, tiled=True, axis_index_groups=groups
        )

    cond_mine = over_plane(conduction).reshape(8, points)
    cond_other = send(cond_mine, CORE)
    cond = jnp.concatenate(
        [
            jnp.where(core == 0, cond_mine, cond_other),
            jnp.where(core == 0, cond_other, cond_mine),
        ],
        axis=0,
    )

    store = valence_store[0]
    piece_a = lax.dynamic_slice_in_dim(store, yz * 16 + core * 8, 8, 0)
    piece_b = lax.dynamic_slice_in_dim(store, yz * 16 + (1 - core) * 8, 8, 0)
    turns = jnp.array([(b // 2 + b % 2) % 2 for b in range(8)])
    pieces = jnp.where(turns[:, None, None] == 1, piece_b[None], piece_a[None])
    panels = lax.all_to_all(pieces, "band", split_axis=0, concat_axis=0, tiled=True)
    chosen = jnp.concatenate(
        [lax.dynamic_slice_in_dim(panels, owners[i], 1, 0)[0] for i in range(2)], axis=0
    )

    energy_c = conduction_energy.reshape(8, 2).T.reshape(16)
    energy_v = jnp.take(valence_energy, owners, axis=0).reshape(2, 8, 2, 8)
    half = (core + turn) % 2
    energy_v = lax.dynamic_index_in_dim(energy_v, half, 2, keepdims=False)
    energy_v = energy_v.transpose(1, 0, 2).reshape(128)
    weight = (4.0 / math.sqrt(4096)) / (energy_c[:, None] - energy_v[None, :])

    weight = weight.reshape(2048, 1)
    root_rows = coulomb_root(gmap_rows)[:, None]
    root_slab = coulomb_root(gmap_slab)[None, :]
    chosen, weight, root_rows, root_slab, cond = lax.optimization_barrier(
        (chosen, weight, root_rows, root_slab, cond)
    )
    mine = over_plane(chosen).reshape(128, points)
    other = send(mine, CORE)

    rho = rho_kernel(zeta_rows, cond, mine, other, root_rows)
    slab_pp = slab_kernel(mine, cond, zeta_slab, weight, root_slab)

    from_down = send(rho, Z_UP)
    from_up = send(rho, Z_DOWN)
    rho_x = send(rho, CORE)
    slab_px = send(slab_pp, X_PAIR)
    slab_yp = send(slab_pp, Y_PAIR)
    slab_yx = send(slab_pp, Y_CROSS)
    far_0 = send(from_down[0], Z_UP)
    far_1 = send(from_up[1], Z_DOWN)
    from_down_x = send(from_down, CORE)
    from_up_x = send(from_up, CORE)
    far_0x = send(far_0, CORE)
    far_1x = send(far_1, CORE)

    near = [rho, rho_x, from_down, from_down_x, from_up, from_up_x]
    near_parts = [((i, i % 2), (i, 1 - i % 2)) for i in range(6)]
    rest = [far_0, far_1, far_0x, far_1x]
    rest_parts = [((0, None), (1, None)), ((3, None), (2, None))]
    near_out = chi_kernel(near, near_parts, slab_yp, slab_yx, BF, "chi_near_out")
    near_in = chi_kernel(near, near_parts, slab_pp, slab_px, F32, "chi_near_in")
    got_near = send(near_out, Y_PAIR)
    rest_out = chi_kernel(rest, rest_parts, slab_yp, slab_yx, BF, "chi_far_out")
    got_rest = send(rest_out, Y_PAIR)
    rest_in = chi_kernel(rest, rest_parts, slab_pp, slab_px, F32, "chi_far_in")

    yl = grow // 8
    z = yz % 4
    own_side, other_side = yl * 4, (1 - yl) * 4
    slots = jnp.stack([z, (z + 3) % 4, (z + 1) % 4]).astype(jnp.int32)
    place_near = jnp.concatenate([own_side + slots, other_side + slots, core[None]])
    opposite = (z + 2) % 4
    place_far = jnp.stack([own_side + opposite, other_side + opposite, core])
    total_rows, cols = chi_prev.shape
    chi = chi_prev.reshape(16, total_rows // 16, cols)
    done = finish_kernel(place_near.astype(jnp.int32), chi, near_in, got_near, None, "finish_near")
    done = finish_kernel(place_far.astype(jnp.int32), chi, rest_in, got_rest, done, "finish_far")
    return done.reshape(total_rows, cols)


def solution(mesh):
    placed = (
        P("band", "grow"),
        P(("band", "grow"), None),
        P("grow", None),
        P("band", None, None),
        P(),
        P("grow", None),
        P(),
        P(),
        P(("band", "grow")),
        P("grow"),
    )
    return jax.shard_map(
        on_device, mesh=mesh, in_specs=placed, out_specs=P("band", "grow"), check_vma=False
    )
```

```python
import math

import jax
import jax.numpy as jnp
from jax import lax
from jax.experimental import pallas as pl
from jax.experimental.pallas import tpu as pltpu
from jax.sharding import PartitionSpec as P

BOX = 64
KC = 2048
VMEM = 56 * 1024 * 1024
BF = jnp.bfloat16
F32 = jnp.float32


def coulomb_root(box_index):
    plane_size = BOX * BOX
    half_box = BOX // 2
    leading = box_index // plane_size
    middle = box_index // BOX % BOX
    trailing = box_index % BOX

    def centred(offset_idx):
        return jnp.where(offset_idx >= half_box, offset_idx - BOX, offset_idx).astype(F32)

    length_sq = centred(leading) ** 2 + centred(middle) ** 2 + centred(trailing) ** 2
    return 32.0 / jnp.sqrt(length_sq + 64.0)


def linear(x, y, z, core):
    return ((x * 2 + y // 2) * 16) + (y % 2) * 8 + z * 2 + core


def route(step):
    pairs = []
    for x in range(4):
        for y in range(4):
            for z in range(4):
                for core in range(2):
                    pairs.append((linear(x, y, z, core), linear(*step(x, y, z, core))))
    return pairs


Z_UP = route(lambda x, y, z, c: (x, y, (z + 1) % 4, c))
Z_DOWN = route(lambda x, y, z, c: (x, y, (z + 3) % 4, c))
CORE = route(lambda x, y, z, c: (x, y, z, 1 - c))
Y_PAIR = route(lambda x, y, z, c: (x, y ^ 1, z, c))
Y_CROSS = route(lambda x, y, z, c: (x, 3 - y, z, c))


def send(value, pairs):
    return lax.ppermute(value, ("band", "grow"), pairs)


def nt_dot(left, right):
    return lax.dot_general(left, right, (((1,), (1,)), ((), ())), preferred_element_type=F32)


def slab_body(val, cond, zeta, weight, root, out, acc):
    step = pl.program_id(0)
    conds = cond.shape[0]
    for c in range(0, conds, 4):
        lhs = jnp.concatenate([val[...] * cond[c + i : c + i + 1, :] for i in range(4)], axis=0)
        part = nt_dot(lhs, zeta[...])
        rows = slice(c * 128, (c + 4) * 128)
        acc[rows] = jnp.where(step == 0, part, acc[rows] + part)

    @pl.when(step == pl.num_programs(0) - 1)
    def _():
        for c in range(conds):
            rows = slice(c * 128, (c + 1) * 128)
            out[rows] = (acc[rows] * root[...] * weight[:, c : c + 1]).astype(BF)


def slab_kernel(val, cond, zeta, weight, root, name):
    conds, points = cond.shape
    pairs = conds * 128
    cols = zeta.shape[0]
    return pl.pallas_call(
        slab_body,
        grid=(points // KC,),
        in_specs=[
            pl.BlockSpec((128, KC), lambda k: (0, k)),
            pl.BlockSpec((conds, KC), lambda k: (0, k)),
            pl.BlockSpec((cols, KC), lambda k: (0, k)),
            pl.BlockSpec((128, conds), lambda k: (0, 0)),
            pl.BlockSpec((1, cols), lambda k: (0, 0)),
        ],
        out_specs=pl.BlockSpec((pairs, cols), lambda k: (0, 0)),
        out_shape=jax.ShapeDtypeStruct((pairs, cols), BF),
        scratch_shapes=[pltpu.VMEM((pairs, cols), F32)],
        compiler_params=pltpu.CompilerParams(vmem_limit_bytes=VMEM),
        cost_estimate=pl.CostEstimate(flops=1 << 20, bytes_accessed=1 << 16, transcendentals=0),
        name=name,
    )(val, cond, zeta, weight, root)


def rho_body(zeta, cond_a, cond_b, val_a, val_b, root, out, lhs, rhs, acc):
    step = pl.program_id(0)
    conds = cond_a.shape[0]
    rows = zeta.shape[0]

    @pl.when(step == 0)
    def _():
        lhs[...] = jnp.zeros_like(lhs)

    rhs[0:128, :] = val_a[...]
    rhs[128:256, :] = val_b[...]
    lhs[0:rows, :] = zeta[...]
    for side, cond in ((0, cond_a), (1, cond_b)):
        for c in range(0, conds, 4):
            left = jnp.concatenate(
                [lhs[...] * cond[c + i : c + i + 1, :] for i in range(4)], axis=0
            )
            part = nt_dot(left, rhs[...])
            first = (side * conds + c) * 128
            span = slice(first, first + 512)
            acc[span] = jnp.where(step == 0, part, acc[span] + part)

    @pl.when(step == pl.num_programs(0) - 1)
    def _():
        for c in range(2 * conds):
            block = acc[c * 128 : c * 128 + rows, :] * root[:, 0:1]
            out[0, :, c * 128 : (c + 1) * 128] = block[:, 0:128].astype(BF)
            out[1, :, c * 128 : (c + 1) * 128] = block[:, 128:256].astype(BF)


def rho_kernel(zeta, cond_a, cond_b, val_a, val_b, root):
    conds, points = cond_a.shape
    rows = zeta.shape[0]
    pairs = 2 * conds * 128
    return pl.pallas_call(
        rho_body,
        grid=(points // KC,),
        in_specs=[
            pl.BlockSpec((rows, KC), lambda k: (0, k)),
            pl.BlockSpec((conds, KC), lambda k: (0, k)),
            pl.BlockSpec((conds, KC), lambda k: (0, k)),
            pl.BlockSpec((128, KC), lambda k: (0, k)),
            pl.BlockSpec((128, KC), lambda k: (0, k)),
            pl.BlockSpec((rows, 128), lambda k: (0, 0)),
        ],
        out_specs=pl.BlockSpec((2, rows, pairs), lambda k: (0, 0, 0)),
        out_shape=jax.ShapeDtypeStruct((2, rows, pairs), BF),
        scratch_shapes=[
            pltpu.VMEM((128, KC), BF),
            pltpu.VMEM((256, KC), BF),
            pltpu.VMEM((pairs, 256), F32),
        ],
        compiler_params=pltpu.CompilerParams(vmem_limit_bytes=VMEM),
        cost_estimate=pl.CostEstimate(flops=1 << 20, bytes_accessed=1 << 16, transcendentals=0),
        name="rho_rows",
    )(zeta, cond_a, cond_b, val_a, val_b, root)


def chi_kernel(parts, sides, name):
    arrays, picks = [], []
    for first, second, crossed in parts:
        pick = []
        for array, index in (first, second):
            known = [i for i, (a, x) in enumerate(arrays) if a is array]
            if not known:
                arrays.append((array, crossed))
                known = [len(arrays) - 1]
            pick.append((known[0], index))
        picks.append(pick)
    rows, depth = arrays[0][0].shape[-2:]
    given, count = len(arrays), len(parts)
    blk = depth // 2
    slabs, found = [], []
    for halves, _ in sides:
        for half in halves:
            found.append([len(slabs), len(slabs) + len(half) - 1])
            slabs += half
    cols = slabs[0].shape[1]

    def body(*refs):
        ins = refs[:given]
        slab_refs = refs[given : given + len(slabs)]
        outs = refs[given + len(slabs) : given + len(slabs) + len(sides)]
        lhs, acc = refs[given + len(slabs) + len(sides) :]
        step = pl.program_id(0)

        @pl.when(step == 0)
        def _():
            lhs[...] = jnp.zeros_like(lhs)

        for half in range(2):
            for i in range(count):
                array, index = picks[i][half]
                block = ins[array][...] if index is None else ins[array][index]
                lhs[half, i * 128 : i * 128 + rows, :] = block

        def product(side, block):
            first, second = found[2 * side][block], found[2 * side + 1][block]
            return jnp.dot(
                lhs[0], slab_refs[first][...], preferred_element_type=F32
            ) + jnp.dot(lhs[1], slab_refs[second][...], preferred_element_type=F32)

        @pl.when(step == 0)
        def _():
            for side in range(len(sides)):
                acc[side] = product(side, 0)

        @pl.when(step == 1)
        def _():
            for side, ref in enumerate(outs):
                total = acc[side] + product(side, 1)
                for i in range(count):
                    ref[i] = total[i * 128 : i * 128 + rows, :].astype(ref.dtype)

    def spec(array, crossed):
        if array.ndim == 3:
            return pl.BlockSpec((2, rows, blk), lambda k: (0, 0, 1 - k if crossed else k))
        return pl.BlockSpec((rows, blk), lambda k: (0, 1 - k if crossed else k))

    def slab_spec(slab):
        if slab.shape[0] == blk:
            return pl.BlockSpec((blk, cols), lambda k: (0, 0))
        return pl.BlockSpec((blk, cols), lambda k: (k, 0))

    whole = pl.BlockSpec((count, rows, cols), lambda k: (0, 0, 0))
    return pl.pallas_call(
        body,
        grid=(2,),
        in_specs=[spec(a, x) for a, x in arrays] + [slab_spec(slab) for slab in slabs],
        out_specs=[whole] * len(sides),
        out_shape=[jax.ShapeDtypeStruct((count, rows, cols), dtype) for _, dtype in sides],
        scratch_shapes=[
            pltpu.VMEM((2, count * 128, blk), BF),
            pltpu.VMEM((len(sides), count * 128, cols), F32),
        ],
        compiler_params=pltpu.CompilerParams(vmem_limit_bytes=VMEM),
        cost_estimate=pl.CostEstimate(flops=1 << 20, bytes_accessed=1 << 16, transcendentals=0),
        name=name,
    )(*[a for a, _ in arrays], *slabs)


def finish_kernel(place, chi, mine, theirs, before, name):
    blocks, rows, cols = chi.shape
    count = mine.shape[0] // 2

    def body(place_ref, chi_ref, mine_ref, theirs_ref, *rest):
        out = rest[-1]
        step = pl.program_id(0)
        core = place_ref[2 * count]
        for first, src in ((0, mine_ref), (count, theirs_ref)):

            @pl.when(jnp.logical_and(step >= first, step < first + count))
            def _(src=src):
                out[core] = chi_ref[core] - src[0].astype(F32)
                out[1 - core] = chi_ref[1 - core] - src[1].astype(F32)

    def where(i, place_ref):
        return (place_ref[i], 0, 0)

    block = (2, rows, cols)
    specs = [
        pl.BlockSpec(block, where),
        pl.BlockSpec(block, lambda i, place_ref: (jnp.minimum(i, count - 1), 0, 0)),
        pl.BlockSpec(block, lambda i, place_ref: (jnp.maximum(i - count, 0), 0, 0)),
    ]
    operands = [place, chi, mine, theirs]
    if before is not None:
        specs.append(pl.BlockSpec(memory_space=pl.ANY))
        operands.append(before)
    return pl.pallas_call(
        body,
        grid_spec=pltpu.PrefetchScalarGridSpec(
            num_scalar_prefetch=1,
            grid=(2 * count,),
            in_specs=specs,
            out_specs=pl.BlockSpec(block, where),
        ),
        out_shape=jax.ShapeDtypeStruct(chi.shape, F32),
        input_output_aliases={} if before is None else {4: 0},
        compiler_params=pltpu.CompilerParams(vmem_limit_bytes=VMEM),
        cost_estimate=pl.CostEstimate(flops=1 << 20, bytes_accessed=1 << 16, transcendentals=0),
        name=name,
    )(*operands)


def on_device(
    chi_prev,
    zeta_rows,
    zeta_slab,
    valence_store,
    valence_energy,
    conduction,
    conduction_energy,
    owners,
    gmap_rows,
    gmap_slab,
):
    band = lax.axis_index("band")
    grow = lax.axis_index("grow")
    core = grow % 2
    yz = grow // 2
    turn = (band // 2 + band % 2) % 2
    points = valence_store.shape[2]

    store = valence_store[0]
    piece_a = lax.dynamic_slice_in_dim(store, yz * 16 + core * 8, 8, 0)
    piece_b = lax.dynamic_slice_in_dim(store, yz * 16 + (1 - core) * 8, 8, 0)
    turns = jnp.array([(b // 2 + b % 2) % 2 for b in range(8)])
    pieces = jnp.where(turns[:, None, None] == 1, piece_b[None], piece_a[None])
    panels = lax.all_to_all(pieces, "band", split_axis=0, concat_axis=0, tiled=True)
    chosen = jnp.concatenate(
        [lax.dynamic_slice_in_dim(panels, owners[i], 1, 0)[0] for i in range(2)], axis=0
    )
    payload = jnp.concatenate([chosen, conduction.reshape(16, points // 16)], axis=1)
    width = payload.shape[1]

    half = (core + turn) % 2
    energy_v = jnp.take(valence_energy, owners, axis=0).reshape(2, 8, 2, 8)
    energy_v = energy_v.transpose(2, 1, 0, 3).reshape(2, 128)
    energy_v = jnp.where(half == 0, energy_v, energy_v[::-1])
    energy_c = conduction_energy.reshape(8, 2).T
    energy_c = jnp.where(core == 0, energy_c, energy_c[::-1])
    norm = 4.0 / math.sqrt(4096)
    weight = [
        [norm / (energy_c[j][None, :] - energy_v[i][:, None]) for j in range(2)] for i in range(2)
    ]
    weight = [[w[0], w[1], jnp.concatenate(w, axis=1)] for w in weight]
    root_rows = jnp.broadcast_to(coulomb_root(gmap_rows)[:, None], (gmap_rows.shape[0], 128))
    root_slab = coulomb_root(gmap_slab)[None, :]
    payload, weight, root_rows, root_slab = lax.optimization_barrier(
        (payload, weight, root_rows, root_slab)
    )

    groups = [list(range(0, 16, 2)), list(range(1, 16, 2))]
    mine = lax.all_to_all(
        jnp.broadcast_to(payload[None], (8, 16, width)),
        "grow",
        split_axis=0,
        concat_axis=0,
        tiled=True,
        axis_index_groups=groups,
    ).reshape(128, width)
    other = send(mine, CORE)
    cond_mine = mine[:, points:].reshape(8, points)
    cond_other = send(cond_mine, CORE)

    own_00 = slab_kernel(mine, cond_mine, zeta_slab, weight[0][0], root_slab, "slab_00")
    own_00, other, cond_other = lax.optimization_barrier((own_00, other, cond_other))
    out_00 = send(own_00, Y_PAIR)
    out_10 = send(own_00, Y_CROSS)
    rho = rho_kernel(zeta_rows, cond_mine, cond_other, mine, other, root_rows)
    rho, cond_other, out_00, out_10 = lax.optimization_barrier((rho, cond_other, out_00, out_10))

    from_down = send(rho, Z_UP)
    from_up = send(rho, Z_DOWN)
    rho_x = send(rho, CORE)
    own_01 = slab_kernel(mine, cond_other, zeta_slab, weight[0][1], root_slab, "slab_01")
    own_01, other = lax.optimization_barrier((own_01, other))
    out_01 = send(own_01, Y_PAIR)
    out_11 = send(own_01, Y_CROSS)
    cond = jnp.concatenate([cond_mine, cond_other], axis=0)
    own_1 = slab_kernel(other, cond, zeta_slab, weight[1][2], root_slab, "slab_1")
    from_down, from_up, rho_x, out_01, out_11, own_1 = lax.optimization_barrier(
        (from_down, from_up, rho_x, out_01, out_11, own_1)
    )
    out_side = ([[out_00, out_01], [out_10, out_11]], BF)
    in_side = ([[own_00, own_01], [own_1]], F32)

    def both(array, crossed):
        if crossed:
            return ((array, 1), (array, 0), True)
        return ((array, 0), (array, 1), False)

    far_0 = send(from_down[0], Z_UP)
    far_1 = send(from_up[1], Z_DOWN)
    from_down_x = send(from_down, CORE)
    from_up_x = send(from_up, CORE)
    near = [both(rho, False), both(rho_x, True)]
    near_out, near_in = chi_kernel(near, [out_side, in_side], "chi_own")
    got_near = send(near_out, Y_PAIR)
    mid = [both(from_down, False), both(from_down_x, True), both(from_up, False), both(from_up_x, True)]
    mid_out, mid_in = chi_kernel(mid, [out_side, in_side], "chi_next")
    got_mid = send(mid_out, Y_PAIR)
    far_0, far_1, near_in, mid_in, got_near = lax.optimization_barrier(
        (far_0, far_1, near_in, mid_in, got_near)
    )

    far_0x = send(far_0, CORE)
    far_1x = send(far_1, CORE)
    far = [((far_0, None), (far_1, None), False), ((far_1x, None), (far_0x, None), True)]
    (far_out,) = chi_kernel(far, [out_side], "chi_far_out")
    got_far = send(far_out, Y_PAIR)
    (far_in,) = chi_kernel(far, [in_side], "chi_far_in")

    yl = grow // 8
    z = yz % 4
    total_rows, cols = chi_prev.shape
    done = None
    chi = chi_prev.reshape(16, total_rows // 16, cols)
    for steps, inner, outer, name in (
        ((0,), near_in, got_near, "finish_own"),
        ((3, 1), mid_in, got_mid, "finish_next"),
        ((2,), far_in, got_far, "finish_far"),
    ):
        slots = jnp.stack([(z + s) % 4 for s in steps])
        place = jnp.concatenate([yl * 4 + slots, (1 - yl) * 4 + slots, core[None]])
        done = finish_kernel(place.astype(jnp.int32), chi, inner, outer, done, name)
    return done.reshape(total_rows, cols)


def solution(mesh):
    placed = (
        P("band", "grow"),
        P(("band", "grow"), None),
        P("grow", None),
        P("band", None, None),
        P(),
        P("grow", None),
        P(),
        P(),
        P(("band", "grow")),
        P("grow"),
    )
    return jax.shard_map(
        on_device, mesh=mesh, in_specs=placed, out_specs=P("band", "grow"), check_vma=False
    )
```

```python
import math

import jax
import jax.numpy as jnp
from jax import lax
from jax.experimental import pallas as pl
from jax.experimental.pallas import tpu as pltpu
from jax.sharding import PartitionSpec as P

BOX = 64
KC = 2048
VMEM = 32 * 1024 * 1024
BF = jnp.bfloat16
F32 = jnp.float32


def coulomb_root(box_index):
    plane_size = BOX * BOX
    half_box = BOX // 2
    leading = box_index // plane_size
    middle = box_index // BOX % BOX
    trailing = box_index % BOX

    def centred(offset_idx):
        return jnp.where(offset_idx >= half_box, offset_idx - BOX, offset_idx).astype(F32)

    length_sq = centred(leading) ** 2 + centred(middle) ** 2 + centred(trailing) ** 2
    return 32.0 / jnp.sqrt(length_sq + 64.0)


def linear(x, y, z, core):
    return ((x * 2 + y // 2) * 16) + (y % 2) * 8 + z * 2 + core


def route(step):
    pairs = []
    for x in range(4):
        for y in range(4):
            for z in range(4):
                for core in range(2):
                    pairs.append((linear(x, y, z, core), linear(*step(x, y, z, core))))
    return pairs


Z_UP = route(lambda x, y, z, c: (x, y, (z + 1) % 4, c))
Z_DOWN = route(lambda x, y, z, c: (x, y, (z + 3) % 4, c))
CORE = route(lambda x, y, z, c: (x, y, z, 1 - c))
Y_PAIR = route(lambda x, y, z, c: (x, y ^ 1, z, c))
Y_CROSS = route(lambda x, y, z, c: (x, 3 - y, z, c))


def send(value, pairs):
    return lax.ppermute(value, ("band", "grow"), pairs)


def nt_dot(left, right):
    return lax.dot_general(left, right, (((1,), (1,)), ((), ())), preferred_element_type=F32)


def slab_body(val, cond, zeta, weight, root, out, acc):
    step = pl.program_id(0)
    conds = cond.shape[0]
    for c in range(0, conds, 4):
        lhs = jnp.concatenate([val[...] * cond[c + i : c + i + 1, :] for i in range(4)], axis=0)
        part = nt_dot(lhs, zeta[...])
        rows = slice(c * 128, (c + 4) * 128)
        acc[rows] = jnp.where(step == 0, part, acc[rows] + part)

    @pl.when(step == pl.num_programs(0) - 1)
    def _():
        for c in range(conds):
            rows = slice(c * 128, (c + 1) * 128)
            out[rows] = (acc[rows] * root[...] * weight[:, c : c + 1]).astype(BF)


def slab_kernel(val, cond, zeta, weight, root, name):
    conds, points = cond.shape
    pairs = conds * 128
    cols = zeta.shape[0]
    return pl.pallas_call(
        slab_body,
        grid=(points // KC,),
        in_specs=[
            pl.BlockSpec((128, KC), lambda k: (0, k)),
            pl.BlockSpec((conds, KC), lambda k: (0, k)),
            pl.BlockSpec((cols, KC), lambda k: (0, k)),
            pl.BlockSpec((128, conds), lambda k: (0, 0)),
            pl.BlockSpec((1, cols), lambda k: (0, 0)),
        ],
        out_specs=pl.BlockSpec((pairs, cols), lambda k: (0, 0)),
        out_shape=jax.ShapeDtypeStruct((pairs, cols), BF),
        scratch_shapes=[pltpu.VMEM((pairs, cols), F32)],
        compiler_params=pltpu.CompilerParams(vmem_limit_bytes=VMEM),
        cost_estimate=pl.CostEstimate(flops=1 << 20, bytes_accessed=1 << 16, transcendentals=0),
        name=name,
    )(val, cond, zeta, weight, root)


def rho_body(zeta, cond, val_a, val_b, root, out, lhs, rhs, acc):
    step = pl.program_id(0)
    conds = cond.shape[0]
    rows = zeta.shape[0]

    @pl.when(step == 0)
    def _():
        lhs[...] = jnp.zeros_like(lhs)

    rhs[0:128, :] = val_a[...]
    rhs[128:256, :] = val_b[...]
    lhs[0:rows, :] = zeta[...]
    for c in range(0, conds, 4):
        left = jnp.concatenate([lhs[...] * cond[c + i : c + i + 1, :] for i in range(4)], axis=0)
        part = nt_dot(left, rhs[...])
        span = slice(c * 128, (c + 4) * 128)
        acc[span] = jnp.where(step == 0, part, acc[span] + part)

    @pl.when(step == pl.num_programs(0) - 1)
    def _():
        for c in range(conds):
            block = acc[c * 128 : c * 128 + rows, :] * root[:, 0:1]
            out[0, :, c * 128 : (c + 1) * 128] = block[:, 0:128].astype(BF)
            out[1, :, c * 128 : (c + 1) * 128] = block[:, 128:256].astype(BF)


def rho_kernel(zeta, cond, val_a, val_b, root, name):
    conds, points = cond.shape
    rows = zeta.shape[0]
    pairs = conds * 128
    return pl.pallas_call(
        rho_body,
        grid=(points // KC,),
        in_specs=[
            pl.BlockSpec((rows, KC), lambda k: (0, k)),
            pl.BlockSpec((conds, KC), lambda k: (0, k)),
            pl.BlockSpec((128, KC), lambda k: (0, k)),
            pl.BlockSpec((128, KC), lambda k: (0, k)),
            pl.BlockSpec((rows, 128), lambda k: (0, 0)),
        ],
        out_specs=pl.BlockSpec((2, rows, pairs), lambda k: (0, 0, 0)),
        out_shape=jax.ShapeDtypeStruct((2, rows, pairs), BF),
        scratch_shapes=[
            pltpu.VMEM((128, KC), BF),
            pltpu.VMEM((256, KC), BF),
            pltpu.VMEM((pairs, 256), F32),
        ],
        compiler_params=pltpu.CompilerParams(vmem_limit_bytes=VMEM),
        cost_estimate=pl.CostEstimate(flops=1 << 20, bytes_accessed=1 << 16, transcendentals=0),
        name=name,
    )(zeta, cond, val_a, val_b, root)


def chi_kernel(parts, sides, name):
    arrays = [array for part in parts for array in part[:2]]
    crossed = [part[2] for part in parts]
    rows, blk = arrays[0].shape[-2:]
    given, count = len(arrays), len(parts)
    slabs = [slab for halves, _ in sides for half in halves for slab in half]
    places, at = [], 0
    for halves, _ in sides:
        for half in halves:
            places.append([(at, 0), (at + len(half) - 1, blk if len(half) == 1 else 0)])
            at += len(half)
    cols = slabs[0].shape[1]

    def body(*refs):
        ins = refs[:given]
        slab_refs = refs[given : given + len(slabs)]
        outs = refs[given + len(slabs) : given + len(slabs) + len(sides)]
        lhs = refs[-1]
        lhs[...] = jnp.zeros_like(lhs)
        totals = [None] * len(sides)
        for side in range(2):
            for half in range(2):
                at = side * 2 + half
                for i in range(count):
                    other = 1 if crossed[i] else 0
                    block = ins[2 * i + (side ^ other)][half ^ other]
                    lhs[at, i * 128 : i * 128 + rows, :] = block
                for which in range(len(sides)):
                    slab, first = places[2 * which + half][side]
                    part = jnp.dot(
                        lhs[at], slab_refs[slab][first : first + blk], preferred_element_type=F32
                    )
                    totals[which] = part if totals[which] is None else totals[which] + part
        for total, out in zip(totals, outs):
            for i in range(count):
                out[i] = total[i * 128 : i * 128 + rows, :].astype(out.dtype)

    return pl.pallas_call(
        body,
        out_shape=[jax.ShapeDtypeStruct((count, rows, cols), dtype) for _, dtype in sides],
        scratch_shapes=[pltpu.VMEM((4, count * 128, blk), BF)],
        compiler_params=pltpu.CompilerParams(vmem_limit_bytes=VMEM),
        cost_estimate=pl.CostEstimate(flops=1 << 20, bytes_accessed=1 << 16, transcendentals=0),
        name=name,
    )(*arrays, *slabs)


def finish_kernel(place, chi, mine, theirs, before, name):
    blocks, rows, cols = chi.shape
    count = mine.shape[0] // 2

    def body(place_ref, chi_ref, mine_ref, theirs_ref, *rest):
        out = rest[-1]
        step = pl.program_id(0)
        core = place_ref[2 * count]
        for first, src in ((0, mine_ref), (count, theirs_ref)):

            @pl.when(jnp.logical_and(step >= first, step < first + count))
            def _(src=src):
                out[core] = chi_ref[core] - src[0].astype(F32)
                out[1 - core] = chi_ref[1 - core] - src[1].astype(F32)

    def where(i, place_ref):
        return (place_ref[i], 0, 0)

    block = (2, rows, cols)
    specs = [
        pl.BlockSpec(block, where),
        pl.BlockSpec(block, lambda i, place_ref: (jnp.minimum(i, count - 1), 0, 0)),
        pl.BlockSpec(block, lambda i, place_ref: (jnp.maximum(i - count, 0), 0, 0)),
    ]
    operands = [place, chi, mine, theirs]
    if before is not None:
        specs.append(pl.BlockSpec(memory_space=pl.ANY))
        operands.append(before)
    return pl.pallas_call(
        body,
        grid_spec=pltpu.PrefetchScalarGridSpec(
            num_scalar_prefetch=1,
            grid=(2 * count,),
            in_specs=specs,
            out_specs=pl.BlockSpec(block, where),
        ),
        out_shape=jax.ShapeDtypeStruct(chi.shape, F32),
        input_output_aliases={} if before is None else {4: 0},
        compiler_params=pltpu.CompilerParams(vmem_limit_bytes=VMEM),
        cost_estimate=pl.CostEstimate(flops=1 << 20, bytes_accessed=1 << 16, transcendentals=0),
        name=name,
    )(*operands)


def on_device(
    chi_prev,
    zeta_rows,
    zeta_slab,
    valence_store,
    valence_energy,
    conduction,
    conduction_energy,
    owners,
    gmap_rows,
    gmap_slab,
):
    band = lax.axis_index("band")
    grow = lax.axis_index("grow")
    core = grow % 2
    yz = grow // 2
    turn = (band // 2 + band % 2) % 2
    points = valence_store.shape[2]

    store = valence_store[0]
    piece_a = lax.dynamic_slice_in_dim(store, yz * 16 + core * 8, 8, 0)
    piece_b = lax.dynamic_slice_in_dim(store, yz * 16 + (1 - core) * 8, 8, 0)
    turns = jnp.array([(b // 2 + b % 2) % 2 for b in range(8)])
    pieces = jnp.where(turns[:, None, None] == 1, piece_b[None], piece_a[None])
    panels = lax.all_to_all(pieces, "band", split_axis=0, concat_axis=0, tiled=True)
    chosen = jnp.concatenate(
        [lax.dynamic_slice_in_dim(panels, owners[i], 1, 0)[0] for i in range(2)], axis=0
    )
    payload = jnp.concatenate([chosen, conduction.reshape(16, points // 16)], axis=1)
    width = payload.shape[1]

    half = (core + turn) % 2
    energy_v = jnp.take(valence_energy, owners, axis=0).reshape(2, 8, 2, 8)
    energy_v = energy_v.transpose(2, 1, 0, 3).reshape(2, 128)
    energy_v = jnp.where(half == 0, energy_v, energy_v[::-1])
    energy_c = conduction_energy.reshape(8, 2).T
    energy_c = jnp.where(core == 0, energy_c, energy_c[::-1])
    norm = 4.0 / math.sqrt(4096)
    weight = [
        [norm / (energy_c[j][None, :] - energy_v[i][:, None]) for j in range(2)] for i in range(2)
    ]
    weight = [[w[0], w[1], jnp.concatenate(w, axis=1)] for w in weight]
    root_rows = jnp.broadcast_to(coulomb_root(gmap_rows)[:, None], (gmap_rows.shape[0], 128))
    root_slab = coulomb_root(gmap_slab)[None, :]
    payload, weight, root_rows, root_slab = lax.optimization_barrier(
        (payload, weight, root_rows, root_slab)
    )

    groups = [list(range(0, 16, 2)), list(range(1, 16, 2))]
    mine = lax.all_to_all(
        jnp.broadcast_to(payload[None], (8, 16, width)),
        "grow",
        split_axis=0,
        concat_axis=0,
        tiled=True,
        axis_index_groups=groups,
    ).reshape(128, width)
    other = send(mine, CORE)
    cond_mine = mine[:, points:].reshape(8, points)
    cond_other = send(cond_mine, CORE)

    own_00 = slab_kernel(mine, cond_mine, zeta_slab, weight[0][0], root_slab, "slab_00")
    own_00, other, cond_other = lax.optimization_barrier((own_00, other, cond_other))
    out_00 = send(own_00, Y_PAIR)
    out_10 = send(own_00, Y_CROSS)

    rho_0 = rho_kernel(zeta_rows, cond_mine, mine, other, root_rows, "rho_0")
    rho_0, cond_other = lax.optimization_barrier((rho_0, cond_other))
    down_0 = send(rho_0, Z_UP)
    up_0 = send(rho_0, Z_DOWN)
    rho_1 = rho_kernel(zeta_rows, cond_other, mine, other, root_rows, "rho_1")
    rho_0x = send(rho_0, CORE)
    rho_1, cond_other, out_00, out_10, rho_0x = lax.optimization_barrier(
        (rho_1, cond_other, out_00, out_10, rho_0x)
    )
    down_1 = send(rho_1, Z_UP)
    up_1 = send(rho_1, Z_DOWN)
    own_01 = slab_kernel(mine, cond_other, zeta_slab, weight[0][1], root_slab, "slab_01")
    rho_1x = send(rho_1, CORE)
    own_01, other, down_0, up_0, rho_1x = lax.optimization_barrier(
        (own_01, other, down_0, up_0, rho_1x)
    )
    far_0 = send(down_0, Z_UP)
    out_01 = send(own_01, Y_PAIR)
    out_11 = send(own_01, Y_CROSS)
    own_10 = slab_kernel(other, cond_mine, zeta_slab, weight[1][0], root_slab, "slab_10")
    own_10, other, down_1, up_1 = lax.optimization_barrier((own_10, other, down_1, up_1))
    far_1 = send(up_1, Z_DOWN)
    own_11 = slab_kernel(other, cond_other, zeta_slab, weight[1][1], root_slab, "slab_11")
    own_11, out_01, out_11, far_0, far_1, down_0, up_0, down_1, up_1 = lax.optimization_barrier(
        (own_11, out_01, out_11, far_0, far_1, down_0, up_0, down_1, up_1)
    )
    out_side = ([[out_00, out_01], [out_10, out_11]], BF)
    in_side = ([[own_00, own_01], [own_10, own_11]], F32)

    near = [(rho_0, rho_1, False), (rho_0x, rho_1x, True)]
    near_out, near_in = chi_kernel(near, [out_side, in_side], "chi_own")
    got_near = send(near_out, Y_PAIR)
    mid = [
        (down_0, down_1, False),
        (send(down_0, CORE), send(down_1, CORE), True),
        (up_0, up_1, False),
        (send(up_0, CORE), send(up_1, CORE), True),
    ]
    mid_out, mid_in = chi_kernel(mid, [out_side, in_side], "chi_next")
    got_mid = send(mid_out, Y_PAIR)
    far_0, far_1, near_in, mid_in, got_near = lax.optimization_barrier(
        (far_0, far_1, near_in, mid_in, got_near)
    )

    far = [(far_0, far_1, False), (send(far_0, CORE), send(far_1, CORE), True)]
    (far_out,) = chi_kernel(far, [out_side], "chi_far_out")
    got_far = send(far_out, Y_PAIR)
    (far_in,) = chi_kernel(far, [in_side], "chi_far_in")

    yl = grow // 8
    z = yz % 4
    total_rows, cols = chi_prev.shape
    done = None
    chi = chi_prev.reshape(16, total_rows // 16, cols)
    for steps, inner, outer, name in (
        ((0,), near_in, got_near, "finish_own"),
        ((3, 1), mid_in, got_mid, "finish_next"),
        ((2,), far_in, got_far, "finish_far"),
    ):
        slots = jnp.stack([(z + s) % 4 for s in steps])
        place = jnp.concatenate([yl * 4 + slots, (1 - yl) * 4 + slots, core[None]])
        done = finish_kernel(place.astype(jnp.int32), chi, inner, outer, done, name)
    return done.reshape(total_rows, cols)


def solution(mesh):
    placed = (
        P("band", "grow"),
        P(("band", "grow"), None),
        P("grow", None),
        P("band", None, None),
        P(),
        P("grow", None),
        P(),
        P(),
        P(("band", "grow")),
        P("grow"),
    )
    return jax.shard_map(
        on_device, mesh=mesh, in_specs=placed, out_specs=P("band", "grow"), check_vma=False
    )
```

```python
import math

import jax
import jax.numpy as jnp
from jax import lax
from jax.experimental import pallas as pl
from jax.experimental.pallas import tpu as pltpu
from jax.sharding import PartitionSpec as P

BOX = 64
KC = 2048
VMEM = 16 * 1024 * 1024
BF = jnp.bfloat16
F32 = jnp.float32


def coulomb_root(box_index):
    plane_size = BOX * BOX
    half_box = BOX // 2
    leading = box_index // plane_size
    middle = box_index // BOX % BOX
    trailing = box_index % BOX

    def centred(offset_idx):
        return jnp.where(offset_idx >= half_box, offset_idx - BOX, offset_idx).astype(F32)

    length_sq = centred(leading) ** 2 + centred(middle) ** 2 + centred(trailing) ** 2
    return 32.0 / jnp.sqrt(length_sq + 64.0)


def linear(x, y, z, core):
    return ((x * 2 + y // 2) * 16) + (y % 2) * 8 + z * 2 + core


def route(step):
    pairs = []
    for x in range(4):
        for y in range(4):
            for z in range(4):
                for core in range(2):
                    pairs.append((linear(x, y, z, core), linear(*step(x, y, z, core))))
    return pairs


Z_UP = route(lambda x, y, z, c: (x, y, (z + 1) % 4, c))
Z_DOWN = route(lambda x, y, z, c: (x, y, (z + 3) % 4, c))
CORE = route(lambda x, y, z, c: (x, y, z, 1 - c))
Y_PAIR = route(lambda x, y, z, c: (x, y ^ 1, z, c))
Y_CROSS = route(lambda x, y, z, c: (x, 3 - y, z, c))


def send(value, pairs):
    return lax.ppermute(value, ("band", "grow"), pairs)


def nt_dot(left, right):
    return lax.dot_general(left, right, (((1,), (1,)), ((), ())), preferred_element_type=F32)


def slab_body(val, cond, zeta, weight, root, out, acc):
    step = pl.program_id(0)
    conds = cond.shape[0]
    for c in range(0, conds, 4):
        lhs = jnp.concatenate([val[...] * cond[c + i : c + i + 1, :] for i in range(4)], axis=0)
        part = nt_dot(lhs, zeta[...])
        rows = slice(c * 128, (c + 4) * 128)
        acc[rows] = jnp.where(step == 0, part, acc[rows] + part)

    @pl.when(step == pl.num_programs(0) - 1)
    def _():
        for c in range(conds):
            rows = slice(c * 128, (c + 1) * 128)
            out[rows] = (acc[rows] * root[...] * weight[:, c : c + 1]).astype(BF)


def slab_kernel(val, cond, zeta, weight, root, name):
    conds, points = cond.shape
    pairs = conds * 128
    cols = zeta.shape[0]
    return pl.pallas_call(
        slab_body,
        grid=(points // KC,),
        in_specs=[
            pl.BlockSpec((128, KC), lambda k: (0, k)),
            pl.BlockSpec((conds, KC), lambda k: (0, k)),
            pl.BlockSpec((cols, KC), lambda k: (0, k)),
            pl.BlockSpec((128, conds), lambda k: (0, 0)),
            pl.BlockSpec((1, cols), lambda k: (0, 0)),
        ],
        out_specs=pl.BlockSpec((pairs, cols), lambda k: (0, 0)),
        out_shape=jax.ShapeDtypeStruct((pairs, cols), BF),
        scratch_shapes=[pltpu.VMEM((pairs, cols), F32)],
        compiler_params=pltpu.CompilerParams(vmem_limit_bytes=VMEM),
        cost_estimate=pl.CostEstimate(flops=1 << 20, bytes_accessed=1 << 16, transcendentals=0),
        name=name,
    )(val, cond, zeta, weight, root)


def rho_body(zeta, cond, val_a, val_b, root, out, lhs, rhs, acc):
    step = pl.program_id(0)
    conds = cond.shape[0]
    rows = zeta.shape[0]

    @pl.when(step == 0)
    def _():
        lhs[...] = jnp.zeros_like(lhs)

    rhs[0:128, :] = val_a[...]
    rhs[128:256, :] = val_b[...]
    lhs[0:rows, :] = zeta[...]
    for c in range(0, conds, 4):
        left = jnp.concatenate([lhs[...] * cond[c + i : c + i + 1, :] for i in range(4)], axis=0)
        part = nt_dot(left, rhs[...])
        span = slice(c * 128, (c + 4) * 128)
        acc[span] = jnp.where(step == 0, part, acc[span] + part)

    @pl.when(step == pl.num_programs(0) - 1)
    def _():
        for c in range(conds):
            block = acc[c * 128 : c * 128 + rows, :] * root[:, 0:1]
            out[0, :, c * 128 : (c + 1) * 128] = block[:, 0:128].astype(BF)
            out[1, :, c * 128 : (c + 1) * 128] = block[:, 128:256].astype(BF)


def rho_kernel(zeta, cond, val_a, val_b, root, name):
    conds, points = cond.shape
    rows = zeta.shape[0]
    pairs = conds * 128
    return pl.pallas_call(
        rho_body,
        grid=(points // KC,),
        in_specs=[
            pl.BlockSpec((rows, KC), lambda k: (0, k)),
            pl.BlockSpec((conds, KC), lambda k: (0, k)),
            pl.BlockSpec((128, KC), lambda k: (0, k)),
            pl.BlockSpec((128, KC), lambda k: (0, k)),
            pl.BlockSpec((rows, 128), lambda k: (0, 0)),
        ],
        out_specs=pl.BlockSpec((2, rows, pairs), lambda k: (0, 0, 0)),
        out_shape=jax.ShapeDtypeStruct((2, rows, pairs), BF),
        scratch_shapes=[
            pltpu.VMEM((128, KC), BF),
            pltpu.VMEM((256, KC), BF),
            pltpu.VMEM((pairs, 256), F32),
        ],
        compiler_params=pltpu.CompilerParams(vmem_limit_bytes=VMEM),
        cost_estimate=pl.CostEstimate(flops=1 << 20, bytes_accessed=1 << 16, transcendentals=0),
        name=name,
    )(zeta, cond, val_a, val_b, root)


def chi_kernel(parts, sides, name):
    arrays = [array for part in parts for array in part[:2]]
    crossed = [part[2] for part in parts]
    rows, blk = arrays[0].shape[-2:]
    given, count = len(arrays), len(parts)
    slabs = [slab for halves, _ in sides for half in halves for slab in half]
    places, at = [], 0
    for halves, _ in sides:
        for half in halves:
            places.append([(at, 0), (at + len(half) - 1, blk if len(half) == 1 else 0)])
            at += len(half)
    cols = slabs[0].shape[1]

    def body(*refs):
        ins = refs[:given]
        slab_refs = refs[given : given + len(slabs)]
        outs = refs[given + len(slabs) : given + len(slabs) + len(sides)]
        lhs = refs[-1]
        lhs[...] = jnp.zeros_like(lhs)
        totals = [None] * len(sides)
        for side in range(2):
            for half in range(2):
                at = side * 2 + half
                for i in range(count):
                    other = 1 if crossed[i] else 0
                    block = ins[2 * i + (side ^ other)][half ^ other]
                    lhs[at, i * 128 : i * 128 + rows, :] = block
                for which in range(len(sides)):
                    slab, first = places[2 * which + half][side]
                    part = jnp.dot(
                        lhs[at], slab_refs[slab][first : first + blk], preferred_element_type=F32
                    )
                    totals[which] = part if totals[which] is None else totals[which] + part
        for total, out in zip(totals, outs):
            for i in range(count):
                out[i] = total[i * 128 : i * 128 + rows, :].astype(out.dtype)

    return pl.pallas_call(
        body,
        out_shape=[jax.ShapeDtypeStruct((count, rows, cols), dtype) for _, dtype in sides],
        scratch_shapes=[pltpu.VMEM((4, count * 128, blk), BF)],
        compiler_params=pltpu.CompilerParams(vmem_limit_bytes=VMEM),
        cost_estimate=pl.CostEstimate(flops=1 << 20, bytes_accessed=1 << 16, transcendentals=0),
        name=name,
    )(*arrays, *slabs)


def finish_kernel(place, chi, sources, before, name):
    _, rows, cols = chi.shape
    counts = [source[4] for source in sources]
    firsts = [sum(counts[:i]) for i in range(len(counts))]

    def body(place_ref, chi_ref, *refs):
        out = refs[-1]
        step = pl.program_id(0)
        core = place_ref[sum(counts)]
        for i, (first, count) in enumerate(zip(firsts, counts)):

            @pl.when(jnp.logical_and(step >= first, step < first + count))
            def _(mine=refs[2 * i], theirs=refs[2 * i + 1]):
                out[core] = chi_ref[core] - mine[0].astype(F32)
                out[1 - core] = chi_ref[1 - core] - theirs[0].astype(F32)

    def where(i, p):
        return (p[i], 0, 0)

    def slot(first, count, start):
        return lambda i, p: (start + jnp.clip(i - first, 0, count - 1), 0, 0)

    specs = [pl.BlockSpec((2, rows, cols), where)]
    operands = [place, chi]
    for (mine, start, theirs, start_x, count), first in zip(sources, firsts):
        specs.append(pl.BlockSpec((1, rows, cols), slot(first, count, start)))
        specs.append(pl.BlockSpec((1, rows, cols), slot(first, count, start_x)))
        operands += [mine, theirs]
    aliases = {}
    if before is not None:
        aliases = {len(operands): 0}
        specs.append(pl.BlockSpec(memory_space=pl.ANY))
        operands.append(before)
    return pl.pallas_call(
        body,
        grid_spec=pltpu.PrefetchScalarGridSpec(
            num_scalar_prefetch=1,
            grid=(sum(counts),),
            in_specs=specs,
            out_specs=pl.BlockSpec((2, rows, cols), where),
        ),
        out_shape=jax.ShapeDtypeStruct(chi.shape, F32),
        input_output_aliases=aliases,
        compiler_params=pltpu.CompilerParams(vmem_limit_bytes=VMEM),
        cost_estimate=pl.CostEstimate(flops=1 << 20, bytes_accessed=1 << 16, transcendentals=0),
        name=name,
    )(*operands)


def on_device(
    chi_prev,
    zeta_rows,
    zeta_slab,
    valence_store,
    valence_energy,
    conduction,
    conduction_energy,
    owners,
    gmap_rows,
    gmap_slab,
):
    band = lax.axis_index("band")
    grow = lax.axis_index("grow")
    core = grow % 2
    yz = grow // 2
    turn = (band // 2 + band % 2) % 2
    points = valence_store.shape[2]

    store = valence_store[0]
    piece_a = lax.dynamic_slice_in_dim(store, yz * 16 + core * 8, 8, 0)
    piece_b = lax.dynamic_slice_in_dim(store, yz * 16 + (1 - core) * 8, 8, 0)
    turns = jnp.array([(b // 2 + b % 2) % 2 for b in range(8)])
    pieces = jnp.where(turns[:, None, None] == 1, piece_b[None], piece_a[None])
    panels = lax.all_to_all(pieces, "band", split_axis=0, concat_axis=0, tiled=True)
    chosen = jnp.concatenate(
        [lax.dynamic_slice_in_dim(panels, owners[i], 1, 0)[0] for i in range(2)], axis=0
    )
    payload = jnp.concatenate([chosen, conduction.reshape(16, points // 16)], axis=1)
    width = payload.shape[1]

    half = (core + turn) % 2
    energy_v = jnp.take(valence_energy, owners, axis=0).reshape(2, 8, 2, 8)
    energy_v = energy_v.transpose(2, 1, 0, 3).reshape(2, 128)
    energy_v = jnp.where(half == 0, energy_v, energy_v[::-1])
    energy_c = conduction_energy.reshape(8, 2).T
    energy_c = jnp.where(core == 0, energy_c, energy_c[::-1])
    norm = 4.0 / math.sqrt(4096)
    weight = [
        [norm / (energy_c[j][None, :] - energy_v[i][:, None]) for j in range(2)] for i in range(2)
    ]
    weight = [[w[0], w[1], jnp.concatenate(w, axis=1)] for w in weight]
    root_rows = jnp.broadcast_to(coulomb_root(gmap_rows)[:, None], (gmap_rows.shape[0], 128))
    root_slab = coulomb_root(gmap_slab)[None, :]
    payload, weight, root_rows, root_slab = lax.optimization_barrier(
        (payload, weight, root_rows, root_slab)
    )

    groups = [list(range(0, 16, 2)), list(range(1, 16, 2))]
    mine = lax.all_to_all(
        jnp.broadcast_to(payload[None], (8, 16, width)),
        "grow",
        split_axis=0,
        concat_axis=0,
        tiled=True,
        axis_index_groups=groups,
    ).reshape(128, width)
    other = send(mine, CORE)
    cond_mine = mine[:, points:].reshape(8, points)
    cond_other = send(cond_mine, CORE)

    own_00 = slab_kernel(mine, cond_mine, zeta_slab, weight[0][0], root_slab, "slab_00")
    own_00, other, cond_other = lax.optimization_barrier((own_00, other, cond_other))
    out_00 = send(own_00, Y_PAIR)
    out_10 = send(own_00, Y_CROSS)

    rho_0 = rho_kernel(zeta_rows, cond_mine, mine, other, root_rows, "rho_0")
    rho_0, cond_other = lax.optimization_barrier((rho_0, cond_other))
    down_0 = send(rho_0, Z_UP)
    up_0 = send(rho_0, Z_DOWN)
    rho_1 = rho_kernel(zeta_rows, cond_other, mine, other, root_rows, "rho_1")
    rho_0x = send(rho_0, CORE)
    rho_1, cond_other, out_00, out_10, rho_0x = lax.optimization_barrier(
        (rho_1, cond_other, out_00, out_10, rho_0x)
    )
    down_1 = send(rho_1, Z_UP)
    up_1 = send(rho_1, Z_DOWN)
    own_01 = slab_kernel(mine, cond_other, zeta_slab, weight[0][1], root_slab, "slab_01")
    rho_1x = send(rho_1, CORE)
    own_01, other, down_0, up_0, rho_1x = lax.optimization_barrier(
        (own_01, other, down_0, up_0, rho_1x)
    )
    far_0 = send(down_0, Z_UP)
    out_01 = send(own_01, Y_PAIR)
    out_11 = send(own_01, Y_CROSS)
    own_10 = slab_kernel(other, cond_mine, zeta_slab, weight[1][0], root_slab, "slab_10")
    own_10, other, down_1, up_1 = lax.optimization_barrier((own_10, other, down_1, up_1))
    far_1 = send(up_1, Z_DOWN)
    own_11 = slab_kernel(other, cond_other, zeta_slab, weight[1][1], root_slab, "slab_11")
    out_side = ([[out_00, out_01], [out_10, out_11]], BF)
    in_side = ([[own_00, own_01], [own_10, own_11]], F32)

    own = [(rho_0, rho_1, False), (rho_0x, rho_1x, True)]
    own_out, own_in = chi_kernel(own, [out_side, in_side], "chi_own")
    got_own = send(own_out, Y_PAIR)
    near = [(down_0, down_1, False), (up_0, up_1, False)]
    near_out, near_in = chi_kernel(near, [out_side, in_side], "chi_near")
    got_near = send(near_out, Y_PAIR)
    own_in, near_in, far_0, far_1, down_0, up_0, down_1, up_1, got_own = lax.optimization_barrier(
        (own_in, near_in, far_0, far_1, down_0, up_0, down_1, up_1, got_own)
    )

    mid = [
        (send(down_0, CORE), send(down_1, CORE), True),
        (send(up_0, CORE), send(up_1, CORE), True),
    ]
    mid_out, mid_in = chi_kernel(mid, [out_side, in_side], "chi_next")
    got_mid = send(mid_out, Y_PAIR)
    far_0x, far_1x = send(far_0, CORE), send(far_1, CORE)
    far_0x, far_1x, mid_in, got_near = lax.optimization_barrier((far_0x, far_1x, mid_in, got_near))
    far = [(far_0, far_1, False), (far_0x, far_1x, True)]
    far_out, far_in = chi_kernel(far, [out_side, in_side], "chi_far")
    got_far = send(far_out, Y_PAIR)

    yl = grow // 8
    z = yz % 4

    def blocks(*pairs):
        return jnp.stack([side * 4 + (z + s) % 4 for side, s in pairs] + [core]).astype(jnp.int32)

    total_rows, cols = chi_prev.shape
    chi = chi_prev.reshape(16, total_rows // 16, cols)
    here, there = yl, 1 - yl
    done = finish_kernel(
        blocks((here, 0), (here, 3), (here, 1), (here, 2), (there, 0), (there, 3), (there, 1)),
        chi,
        [
            (own_in, 0, own_in, 1, 1),
            (near_in, 0, mid_in, 0, 2),
            (far_in, 0, far_in, 1, 1),
            (got_own, 0, got_own, 1, 1),
            (got_near, 0, got_mid, 0, 2),
        ],
        None,
        "finish_most",
    )
    done = finish_kernel(
        blocks((there, 2)), chi, [(got_far, 0, got_far, 1, 1)], done, "finish_far"
    )
    return done.reshape(total_rows, cols)


def solution(mesh):
    placed = (
        P("band", "grow"),
        P(("band", "grow"), None),
        P("grow", None),
        P("band", None, None),
        P(),
        P("grow", None),
        P(),
        P(),
        P(("band", "grow")),
        P("grow"),
    )
    return jax.shard_map(
        on_device, mesh=mesh, in_specs=placed, out_specs=P("band", "grow"), check_vma=False
    )
```

```python
import math

import jax
import jax.numpy as jnp
from jax import lax
from jax.experimental import pallas as pl
from jax.experimental.pallas import tpu as pltpu
from jax.sharding import PartitionSpec as P

BOX = 64
GROUP = 4
VMEM = 32 * 1024 * 1024
BF = jnp.bfloat16
F32 = jnp.float32


def coulomb_root(box_index):
    plane_size = BOX * BOX
    half_box = BOX // 2
    leading = box_index // plane_size
    middle = box_index // BOX % BOX
    trailing = box_index % BOX

    def centred(offset_idx):
        return jnp.where(offset_idx >= half_box, offset_idx - BOX, offset_idx).astype(F32)

    length_sq = centred(leading) ** 2 + centred(middle) ** 2 + centred(trailing) ** 2
    return 32.0 / jnp.sqrt(length_sq + 64.0)


def linear(x, y, z, core):
    return ((x * 2 + y // 2) * 16) + (y % 2) * 8 + z * 2 + core


def route(step):
    pairs = []
    for x in range(4):
        for y in range(4):
            for z in range(4):
                for core in range(2):
                    pairs.append((linear(x, y, z, core), linear(*step(x, y, z, core))))
    return pairs


Z_UP = route(lambda x, y, z, c: (x, y, (z + 1) % 4, c))
Z_DOWN = route(lambda x, y, z, c: (x, y, (z + 3) % 4, c))
CORE = route(lambda x, y, z, c: (x, y, z, 1 - c))
Y_PAIR = route(lambda x, y, z, c: (x, y ^ 1, z, c))
Y_CROSS = route(lambda x, y, z, c: (x, 3 - y, z, c))


def send(value, pairs):
    return lax.ppermute(value, ("band", "grow"), pairs)


def nt_dot(left, right):
    return lax.dot_general(left, right, (((1,), (1,)), ((), ())), preferred_element_type=F32)


def slab_body(val, cond, zeta, weight, root, out):
    conds, points = cond.shape
    for c in range(0, conds, GROUP):
        left = jnp.concatenate(
            [val[:, :points] * cond[c + i : c + i + 1, :] for i in range(GROUP)], axis=0
        )
        part = nt_dot(left, zeta[...])
        for i in range(GROUP):
            at = c + i
            block = part[i * 128 : (i + 1) * 128] * root[...] * weight[:, at : at + 1]
            out[at * 128 : (at + 1) * 128] = block.astype(BF)


def slab_kernel(val, cond, zeta, weight, root, name):
    conds, points = cond.shape
    pairs = conds * 128
    cols = zeta.shape[0]
    return pl.pallas_call(
        slab_body,
        grid=(1,),
        in_specs=[
            pl.BlockSpec((128, points), lambda k: (0, 0)),
            pl.BlockSpec((conds, points), lambda k: (0, 0)),
            pl.BlockSpec((cols, points), lambda k: (0, 0)),
            pl.BlockSpec((128, conds), lambda k: (0, 0)),
            pl.BlockSpec((1, cols), lambda k: (0, 0)),
        ],
        out_specs=pl.BlockSpec((pairs, cols), lambda k: (0, 0)),
        out_shape=jax.ShapeDtypeStruct((pairs, cols), BF),
        compiler_params=pltpu.CompilerParams(vmem_limit_bytes=VMEM),
        cost_estimate=pl.CostEstimate(flops=1 << 20, bytes_accessed=1 << 16, transcendentals=0),
        name=name,
    )(val, cond, zeta, weight, root)


def rho_body(zeta, cond, val_a, val_b, root, out, lhs, rhs):
    conds = cond.shape[0]
    rows = zeta.shape[0]
    lhs[...] = jnp.zeros_like(lhs)
    rhs[0:128, :] = val_a[...]
    rhs[128:256, :] = val_b[...]
    lhs[0:rows, :] = zeta[...]
    for c in range(0, conds, GROUP):
        left = jnp.concatenate(
            [lhs[...] * cond[c + i : c + i + 1, :] for i in range(GROUP)], axis=0
        )
        part = nt_dot(left, rhs[...])
        for i in range(GROUP):
            block = part[i * 128 : i * 128 + rows, :] * root[:, 0:1]
            at = slice((c + i) * 128, (c + i + 1) * 128)
            out[0, :, at] = block[:, 0:128].astype(BF)
            out[1, :, at] = block[:, 128:256].astype(BF)


def rho_kernel(zeta, cond, val_a, val_b, root, name):
    conds, points = cond.shape
    rows = zeta.shape[0]
    pairs = conds * 128
    return pl.pallas_call(
        rho_body,
        grid=(1,),
        in_specs=[
            pl.BlockSpec((rows, points), lambda k: (0, 0)),
            pl.BlockSpec((conds, points), lambda k: (0, 0)),
            pl.BlockSpec((128, points), lambda k: (0, 0)),
            pl.BlockSpec((128, points), lambda k: (0, 0)),
            pl.BlockSpec((rows, 128), lambda k: (0, 0)),
        ],
        out_specs=pl.BlockSpec((2, rows, pairs), lambda k: (0, 0, 0)),
        out_shape=jax.ShapeDtypeStruct((2, rows, pairs), BF),
        scratch_shapes=[pltpu.VMEM((128, points), BF), pltpu.VMEM((256, points), BF)],
        compiler_params=pltpu.CompilerParams(vmem_limit_bytes=VMEM),
        cost_estimate=pl.CostEstimate(flops=1 << 20, bytes_accessed=1 << 16, transcendentals=0),
        name=name,
    )(zeta, cond, val_a, val_b, root)


def chi_kernel(parts, sides, name):
    arrays = [array for part in parts for array in part[:2]]
    crossed = [part[2] for part in parts]
    rows, blk = arrays[0].shape[-2:]
    given, count = len(arrays), len(parts)
    slabs = [slab for halves, _ in sides for half in halves for slab in half]
    places, at = [], 0
    for halves, _ in sides:
        for half in halves:
            places.append([(at, 0), (at + len(half) - 1, blk if len(half) == 1 else 0)])
            at += len(half)
    cols = slabs[0].shape[1]

    def body(*refs):
        ins = refs[:given]
        slab_refs = refs[given : given + len(slabs)]
        outs = refs[given + len(slabs) : given + len(slabs) + len(sides)]
        lhs = refs[-1]
        lhs[...] = jnp.zeros_like(lhs)
        totals = [None] * len(sides)
        for side in range(2):
            for half in range(2):
                at = side * 2 + half
                for i in range(count):
                    other = 1 if crossed[i] else 0
                    block = ins[2 * i + (side ^ other)][half ^ other]
                    lhs[at, i * 128 : i * 128 + rows, :] = block
                for which in range(len(sides)):
                    slab, first = places[2 * which + half][side]
                    part = jnp.dot(
                        lhs[at], slab_refs[slab][first : first + blk], preferred_element_type=F32
                    )
                    totals[which] = part if totals[which] is None else totals[which] + part
        for total, out in zip(totals, outs):
            for i in range(count):
                out[i] = total[i * 128 : i * 128 + rows, :].astype(out.dtype)

    return pl.pallas_call(
        body,
        out_shape=[jax.ShapeDtypeStruct((count, rows, cols), dtype) for _, dtype in sides],
        scratch_shapes=[pltpu.VMEM((4, count * 128, blk), BF)],
        compiler_params=pltpu.CompilerParams(vmem_limit_bytes=VMEM),
        cost_estimate=pl.CostEstimate(flops=1 << 20, bytes_accessed=1 << 16, transcendentals=0),
        name=name,
    )(*arrays, *slabs)


def finish_kernel(place, chi, sources, before, name):
    _, rows, cols = chi.shape
    counts = [source[4] for source in sources]
    firsts = [sum(counts[:i]) for i in range(len(counts))]

    def body(place_ref, chi_ref, *refs):
        out = refs[-1]
        step = pl.program_id(0)
        core = place_ref[sum(counts)]
        for i, (first, count) in enumerate(zip(firsts, counts)):

            @pl.when(jnp.logical_and(step >= first, step < first + count))
            def _(mine=refs[2 * i], theirs=refs[2 * i + 1]):
                out[core] = chi_ref[core] - mine[0].astype(F32)
                out[1 - core] = chi_ref[1 - core] - theirs[0].astype(F32)

    def where(i, p):
        return (p[i], 0, 0)

    def slot(first, count, start):
        return lambda i, p: (start + jnp.clip(i - first, 0, count - 1), 0, 0)

    specs = [pl.BlockSpec((2, rows, cols), where)]
    operands = [place, chi]
    for (mine, start, theirs, start_x, count), first in zip(sources, firsts):
        specs.append(pl.BlockSpec((1, rows, cols), slot(first, count, start)))
        specs.append(pl.BlockSpec((1, rows, cols), slot(first, count, start_x)))
        operands += [mine, theirs]
    aliases = {}
    if before is not None:
        aliases = {len(operands): 0}
        specs.append(pl.BlockSpec(memory_space=pl.ANY))
        operands.append(before)
    return pl.pallas_call(
        body,
        grid_spec=pltpu.PrefetchScalarGridSpec(
            num_scalar_prefetch=1,
            grid=(sum(counts),),
            in_specs=specs,
            out_specs=pl.BlockSpec((2, rows, cols), where),
        ),
        out_shape=jax.ShapeDtypeStruct(chi.shape, F32),
        input_output_aliases=aliases,
        compiler_params=pltpu.CompilerParams(vmem_limit_bytes=VMEM),
        cost_estimate=pl.CostEstimate(flops=1 << 20, bytes_accessed=1 << 16, transcendentals=0),
        name=name,
    )(*operands)


def on_device(
    chi_prev,
    zeta_rows,
    zeta_slab,
    valence_store,
    valence_energy,
    conduction,
    conduction_energy,
    owners,
    gmap_rows,
    gmap_slab,
):
    band = lax.axis_index("band")
    grow = lax.axis_index("grow")
    core = grow % 2
    yz = grow // 2
    turn = (band // 2 + band % 2) % 2
    points = valence_store.shape[2]

    store = valence_store[0]
    piece_a = lax.dynamic_slice_in_dim(store, yz * 16 + core * 8, 8, 0)
    piece_b = lax.dynamic_slice_in_dim(store, yz * 16 + (1 - core) * 8, 8, 0)
    turns = jnp.array([(b // 2 + b % 2) % 2 for b in range(8)])
    pieces = jnp.where(turns[:, None, None] == 1, piece_b[None], piece_a[None])
    panels = lax.all_to_all(pieces, "band", split_axis=0, concat_axis=0, tiled=True)
    chosen = jnp.concatenate(
        [lax.dynamic_slice_in_dim(panels, owners[i], 1, 0)[0] for i in range(2)], axis=0
    )
    payload = jnp.concatenate([chosen, conduction.reshape(16, points // 16)], axis=1)
    width = payload.shape[1]

    half = (core + turn) % 2
    energy_v = jnp.take(valence_energy, owners, axis=0).reshape(2, 8, 2, 8)
    energy_v = energy_v.transpose(2, 1, 0, 3).reshape(2, 128)
    energy_v = jnp.where(half == 0, energy_v, energy_v[::-1])
    energy_c = conduction_energy.reshape(8, 2).T
    energy_c = jnp.where(core == 0, energy_c, energy_c[::-1])
    norm = 4.0 / math.sqrt(4096)
    weight = [
        [norm / (energy_c[j][None, :] - energy_v[i][:, None]) for j in range(2)] for i in range(2)
    ]
    weight = [[w[0], w[1], jnp.concatenate(w, axis=1)] for w in weight]
    root_rows = jnp.broadcast_to(coulomb_root(gmap_rows)[:, None], (gmap_rows.shape[0], 128))
    root_slab = coulomb_root(gmap_slab)[None, :]
    payload, weight, root_rows, root_slab = lax.optimization_barrier(
        (payload, weight, root_rows, root_slab)
    )

    groups = [list(range(0, 16, 2)), list(range(1, 16, 2))]
    mine = lax.all_to_all(
        jnp.broadcast_to(payload[None], (8, 16, width)),
        "grow",
        split_axis=0,
        concat_axis=0,
        tiled=True,
        axis_index_groups=groups,
    ).reshape(128, width)
    other = send(mine, CORE)
    cond_mine = mine[:, points:].reshape(8, points)
    cond_other = send(cond_mine, CORE)

    own_00 = slab_kernel(mine, cond_mine, zeta_slab, weight[0][0], root_slab, "slab_00")
    own_00, other, cond_other = lax.optimization_barrier((own_00, other, cond_other))
    out_00 = send(own_00, Y_PAIR)
    out_10 = send(own_00, Y_CROSS)

    rho_0 = rho_kernel(zeta_rows, cond_mine, mine, other, root_rows, "rho_0")
    rho_0, cond_other = lax.optimization_barrier((rho_0, cond_other))
    down_0 = send(rho_0, Z_UP)
    up_0 = send(rho_0, Z_DOWN)
    rho_1 = rho_kernel(zeta_rows, cond_other, mine, other, root_rows, "rho_1")
    rho_0x = send(rho_0, CORE)
    rho_1, cond_other, out_00, out_10, rho_0x = lax.optimization_barrier(
        (rho_1, cond_other, out_00, out_10, rho_0x)
    )
    down_1 = send(rho_1, Z_UP)
    up_1 = send(rho_1, Z_DOWN)
    own_01 = slab_kernel(mine, cond_other, zeta_slab, weight[0][1], root_slab, "slab_01")
    rho_1x = send(rho_1, CORE)
    own_01, other, down_0, up_0, rho_1x = lax.optimization_barrier(
        (own_01, other, down_0, up_0, rho_1x)
    )
    far_0 = send(down_0, Z_UP)
    out_01 = send(own_01, Y_PAIR)
    out_11 = send(own_01, Y_CROSS)
    own_10 = slab_kernel(other, cond_mine, zeta_slab, weight[1][0], root_slab, "slab_10")
    own_10, other, down_1, up_1 = lax.optimization_barrier((own_10, other, down_1, up_1))
    far_1 = send(up_1, Z_DOWN)
    own_11 = slab_kernel(other, cond_other, zeta_slab, weight[1][1], root_slab, "slab_11")
    out_side = ([[out_00, out_01], [out_10, out_11]], BF)
    in_side = ([[own_00, own_01], [own_10, own_11]], F32)

    own = [(rho_0, rho_1, False), (rho_0x, rho_1x, True)]
    own_out, own_in = chi_kernel(own, [out_side, in_side], "chi_own")
    got_own = send(own_out, Y_PAIR)
    near = [(down_0, down_1, False), (up_0, up_1, False)]
    near_out, near_in = chi_kernel(near, [out_side, in_side], "chi_near")
    got_near = send(near_out, Y_PAIR)
    own_in, near_in, far_0, far_1, down_0, up_0, down_1, up_1, got_own = lax.optimization_barrier(
        (own_in, near_in, far_0, far_1, down_0, up_0, down_1, up_1, got_own)
    )

    mid = [
        (send(down_0, CORE), send(down_1, CORE), True),
        (send(up_0, CORE), send(up_1, CORE), True),
    ]
    mid_out, mid_in = chi_kernel(mid, [out_side, in_side], "chi_next")
    got_mid = send(mid_out, Y_PAIR)
    far_0x, far_1x = send(far_0, CORE), send(far_1, CORE)
    far_0x, far_1x, mid_in, got_near = lax.optimization_barrier((far_0x, far_1x, mid_in, got_near))
    far = [(far_0, far_1, False), (far_0x, far_1x, True)]
    far_out, far_in = chi_kernel(far, [out_side, in_side], "chi_far")
    got_far = send(far_out, Y_PAIR)

    yl = grow // 8
    z = yz % 4

    def blocks(*pairs):
        return jnp.stack([side * 4 + (z + s) % 4 for side, s in pairs] + [core]).astype(jnp.int32)

    total_rows, cols = chi_prev.shape
    chi = chi_prev.reshape(16, total_rows // 16, cols)
    here, there = yl, 1 - yl
    done = finish_kernel(
        blocks((here, 0), (here, 3), (here, 1), (here, 2), (there, 0), (there, 3), (there, 1)),
        chi,
        [
            (own_in, 0, own_in, 1, 1),
            (near_in, 0, mid_in, 0, 2),
            (far_in, 0, far_in, 1, 1),
            (got_own, 0, got_own, 1, 1),
            (got_near, 0, got_mid, 0, 2),
        ],
        None,
        "finish_most",
    )
    done = finish_kernel(
        blocks((there, 2)), chi, [(got_far, 0, got_far, 1, 1)], done, "finish_far"
    )
    return done.reshape(total_rows, cols)


def solution(mesh):
    placed = (
        P("band", "grow"),
        P(("band", "grow"), None),
        P("grow", None),
        P("band", None, None),
        P(),
        P("grow", None),
        P(),
        P(),
        P(("band", "grow")),
        P("grow"),
    )
    return jax.shard_map(
        on_device, mesh=mesh, in_specs=placed, out_specs=P("band", "grow"), check_vma=False
    )
```

```python
import math

import jax
import jax.numpy as jnp
from jax import lax
from jax.experimental import pallas as pl
from jax.experimental.pallas import tpu as pltpu
from jax.sharding import PartitionSpec as P

BOX = 64
GROUP = 4
VMEM = 32 * 1024 * 1024
SMALL = 16 * 1024 * 1024
BF = jnp.bfloat16
F32 = jnp.float32


def coulomb_root(box_index):
    plane_size = BOX * BOX
    half_box = BOX // 2
    leading = box_index // plane_size
    middle = box_index // BOX % BOX
    trailing = box_index % BOX

    def centred(offset_idx):
        return jnp.where(offset_idx >= half_box, offset_idx - BOX, offset_idx).astype(F32)

    length_sq = centred(leading) ** 2 + centred(middle) ** 2 + centred(trailing) ** 2
    return 32.0 / jnp.sqrt(length_sq + 64.0)


def linear(x, y, z, core):
    return ((x * 2 + y // 2) * 16) + (y % 2) * 8 + z * 2 + core


def route(step):
    pairs = []
    for x in range(4):
        for y in range(4):
            for z in range(4):
                for core in range(2):
                    pairs.append((linear(x, y, z, core), linear(*step(x, y, z, core))))
    return pairs


Z_UP = route(lambda x, y, z, c: (x, y, (z + 1) % 4, c))
Z_DOWN = route(lambda x, y, z, c: (x, y, (z + 3) % 4, c))
CORE = route(lambda x, y, z, c: (x, y, z, 1 - c))
Y_PAIR = route(lambda x, y, z, c: (x, y ^ 1, z, c))
Y_CROSS = route(lambda x, y, z, c: (x, 3 - y, z, c))


def send(value, pairs):
    return lax.ppermute(value, ("band", "grow"), pairs)


def nt_dot(left, right):
    return lax.dot_general(left, right, (((1,), (1,)), ((), ())), preferred_element_type=F32)


def slab_body(val, cond, zeta, weight, root, out):
    conds, points = cond.shape
    for c in range(0, conds, GROUP):
        left = jnp.concatenate(
            [val[:, :points] * cond[c + i : c + i + 1, :] for i in range(GROUP)], axis=0
        )
        part = nt_dot(left, zeta[...])
        for i in range(GROUP):
            at = c + i
            block = part[i * 128 : (i + 1) * 128] * root[...] * weight[:, at : at + 1]
            out[at * 128 : (at + 1) * 128] = block.astype(BF)


def slab_kernel(val, cond, zeta, weight, root, name):
    conds, points = cond.shape
    pairs = conds * 128
    cols = zeta.shape[0]
    return pl.pallas_call(
        slab_body,
        grid=(1,),
        in_specs=[
            pl.BlockSpec((128, points), lambda k: (0, 0)),
            pl.BlockSpec((conds, points), lambda k: (0, 0)),
            pl.BlockSpec((cols, points), lambda k: (0, 0)),
            pl.BlockSpec((128, conds), lambda k: (0, 0)),
            pl.BlockSpec((1, cols), lambda k: (0, 0)),
        ],
        out_specs=pl.BlockSpec((pairs, cols), lambda k: (0, 0)),
        out_shape=jax.ShapeDtypeStruct((pairs, cols), BF),
        compiler_params=pltpu.CompilerParams(vmem_limit_bytes=VMEM),
        cost_estimate=pl.CostEstimate(flops=1 << 20, bytes_accessed=1 << 16, transcendentals=0),
        name=name,
    )(val, cond, zeta, weight, root)


def rho_body(zeta, cond, val_a, val_b, root, out, lhs, rhs):
    conds = cond.shape[0]
    rows = zeta.shape[0]
    lhs[...] = jnp.zeros_like(lhs)
    rhs[0:128, :] = val_a[...]
    rhs[128:256, :] = val_b[...]
    lhs[0:rows, :] = zeta[...]
    for c in range(0, conds, GROUP):
        left = jnp.concatenate(
            [lhs[...] * cond[c + i : c + i + 1, :] for i in range(GROUP)], axis=0
        )
        part = nt_dot(left, rhs[...])
        for i in range(GROUP):
            block = part[i * 128 : i * 128 + rows, :] * root[:, 0:1]
            at = slice((c + i) * 128, (c + i + 1) * 128)
            out[0, :, at] = block[:, 0:128].astype(BF)
            out[1, :, at] = block[:, 128:256].astype(BF)


def rho_kernel(zeta, cond, val_a, val_b, root, name):
    conds, points = cond.shape
    rows = zeta.shape[0]
    pairs = conds * 128
    return pl.pallas_call(
        rho_body,
        grid=(1,),
        in_specs=[
            pl.BlockSpec((rows, points), lambda k: (0, 0)),
            pl.BlockSpec((conds, points), lambda k: (0, 0)),
            pl.BlockSpec((128, points), lambda k: (0, 0)),
            pl.BlockSpec((128, points), lambda k: (0, 0)),
            pl.BlockSpec((rows, 128), lambda k: (0, 0)),
        ],
        out_specs=pl.BlockSpec((2, rows, pairs), lambda k: (0, 0, 0)),
        out_shape=jax.ShapeDtypeStruct((2, rows, pairs), BF),
        scratch_shapes=[pltpu.VMEM((128, points), BF), pltpu.VMEM((256, points), BF)],
        compiler_params=pltpu.CompilerParams(vmem_limit_bytes=VMEM),
        cost_estimate=pl.CostEstimate(flops=1 << 20, bytes_accessed=1 << 16, transcendentals=0),
        name=name,
    )(zeta, cond, val_a, val_b, root)


def chi_kernel(parts, sides, name):
    arrays = [array for part in parts for array in part[:2]]
    crossed = [part[2] for part in parts]
    rows, blk = arrays[0].shape[-2:]
    given, count = len(arrays), len(parts)
    slabs = [slab for halves, _ in sides for half in halves for slab in half]
    places, at = [], 0
    for halves, _ in sides:
        for half in halves:
            places.append([(at, 0), (at + len(half) - 1, blk if len(half) == 1 else 0)])
            at += len(half)
    cols = slabs[0].shape[1]

    def body(*refs):
        ins = refs[:given]
        slab_refs = refs[given : given + len(slabs)]
        outs = refs[given + len(slabs) : given + len(slabs) + len(sides)]
        lhs = refs[-1]
        lhs[...] = jnp.zeros_like(lhs)
        totals = [None] * len(sides)
        for side in range(2):
            for half in range(2):
                at = side * 2 + half
                for i in range(count):
                    other = 1 if crossed[i] else 0
                    block = ins[2 * i + (side ^ other)][half ^ other]
                    lhs[at, i * 128 : i * 128 + rows, :] = block
                for which in range(len(sides)):
                    slab, first = places[2 * which + half][side]
                    part = jnp.dot(
                        lhs[at], slab_refs[slab][first : first + blk], preferred_element_type=F32
                    )
                    totals[which] = part if totals[which] is None else totals[which] + part
        for total, out in zip(totals, outs):
            for i in range(count):
                out[i] = total[i * 128 : i * 128 + rows, :].astype(out.dtype)

    return pl.pallas_call(
        body,
        out_shape=[jax.ShapeDtypeStruct((count, rows, cols), dtype) for _, dtype in sides],
        scratch_shapes=[pltpu.VMEM((4, count * 128, blk), BF)],
        compiler_params=pltpu.CompilerParams(vmem_limit_bytes=SMALL),
        cost_estimate=pl.CostEstimate(flops=1 << 20, bytes_accessed=1 << 16, transcendentals=0),
        name=name,
    )(*arrays, *slabs)


def finish_kernel(place, chi, sources, before, name):
    _, rows, cols = chi.shape
    counts = [source[4] for source in sources]
    firsts = [sum(counts[:i]) for i in range(len(counts))]

    def body(place_ref, chi_ref, *refs):
        out = refs[-1]
        step = pl.program_id(0)
        core = place_ref[sum(counts)]
        for i, (first, count) in enumerate(zip(firsts, counts)):

            @pl.when(jnp.logical_and(step >= first, step < first + count))
            def _(mine=refs[2 * i], theirs=refs[2 * i + 1]):
                out[core] = chi_ref[core] - mine[0].astype(F32)
                out[1 - core] = chi_ref[1 - core] - theirs[0].astype(F32)

    def where(i, p):
        return (p[i], 0, 0)

    def slot(first, count, start):
        return lambda i, p: (start + jnp.clip(i - first, 0, count - 1), 0, 0)

    specs = [pl.BlockSpec((2, rows, cols), where)]
    operands = [place, chi]
    for (mine, start, theirs, start_x, count), first in zip(sources, firsts):
        specs.append(pl.BlockSpec((1, rows, cols), slot(first, count, start)))
        specs.append(pl.BlockSpec((1, rows, cols), slot(first, count, start_x)))
        operands += [mine, theirs]
    aliases = {}
    if before is not None:
        aliases = {len(operands): 0}
        specs.append(pl.BlockSpec(memory_space=pl.ANY))
        operands.append(before)
    return pl.pallas_call(
        body,
        grid_spec=pltpu.PrefetchScalarGridSpec(
            num_scalar_prefetch=1,
            grid=(sum(counts),),
            in_specs=specs,
            out_specs=pl.BlockSpec((2, rows, cols), where),
        ),
        out_shape=jax.ShapeDtypeStruct(chi.shape, F32),
        input_output_aliases=aliases,
        compiler_params=pltpu.CompilerParams(vmem_limit_bytes=SMALL),
        cost_estimate=pl.CostEstimate(flops=1 << 20, bytes_accessed=1 << 16, transcendentals=0),
        name=name,
    )(*operands)


def on_device(
    chi_prev,
    zeta_rows,
    zeta_slab,
    valence_store,
    valence_energy,
    conduction,
    conduction_energy,
    owners,
    gmap_rows,
    gmap_slab,
):
    band = lax.axis_index("band")
    grow = lax.axis_index("grow")
    core = grow % 2
    yz = grow // 2
    turn = (band // 2 + band % 2) % 2
    points = valence_store.shape[2]

    store = valence_store[0]
    both_cores = lax.dynamic_slice_in_dim(store, yz * 16, 16, 0).reshape(2, 8, points)
    turns = jnp.array([(b // 2 + b % 2) % 2 for b in range(8)])
    first = ((turns + core) % 2 == 0)[:, None, None]
    pieces = jnp.where(first, both_cores[0][None], both_cores[1][None])
    panels = lax.all_to_all(pieces, "band", split_axis=0, concat_axis=0, tiled=True)
    chosen = jnp.concatenate(
        [lax.dynamic_slice_in_dim(panels, owners[i], 1, 0)[0] for i in range(2)], axis=0
    )
    payload = jnp.concatenate([chosen, conduction.reshape(16, points // 16)], axis=1)
    width = payload.shape[1]

    half = (core + turn) % 2
    energy_v = jnp.take(valence_energy, owners, axis=0).reshape(2, 8, 2, 8)
    energy_v = energy_v.transpose(2, 1, 0, 3).reshape(2, 128)
    energy_v = jnp.where(half == 0, energy_v, energy_v[::-1])
    energy_c = conduction_energy.reshape(8, 2).T
    energy_c = jnp.where(core == 0, energy_c, energy_c[::-1])
    norm = 4.0 / math.sqrt(4096)
    weight = [
        [norm / (energy_c[j][None, :] - energy_v[i][:, None]) for j in range(2)] for i in range(2)
    ]
    weight = [[w[0], w[1], jnp.concatenate(w, axis=1)] for w in weight]
    root_rows = jnp.broadcast_to(coulomb_root(gmap_rows)[:, None], (gmap_rows.shape[0], 128))
    root_slab = coulomb_root(gmap_slab)[None, :]
    payload, weight, root_rows, root_slab = lax.optimization_barrier(
        (payload, weight, root_rows, root_slab)
    )

    groups = [list(range(0, 16, 2)), list(range(1, 16, 2))]
    mine = lax.all_to_all(
        jnp.broadcast_to(payload[None], (8, 16, width)),
        "grow",
        split_axis=0,
        concat_axis=0,
        tiled=True,
        axis_index_groups=groups,
    ).reshape(128, width)
    other = send(mine, CORE)
    cond_mine = mine[:, points:].reshape(8, points)
    cond_other = send(cond_mine, CORE)

    own_00 = slab_kernel(mine, cond_mine, zeta_slab, weight[0][0], root_slab, "slab_00")
    own_00, other, cond_other = lax.optimization_barrier((own_00, other, cond_other))
    out_00 = send(own_00, Y_PAIR)
    out_10 = send(own_00, Y_CROSS)

    rho_0 = rho_kernel(zeta_rows, cond_mine, mine, other, root_rows, "rho_0")
    rho_0, cond_other = lax.optimization_barrier((rho_0, cond_other))
    down_0 = send(rho_0, Z_UP)
    up_0 = send(rho_0, Z_DOWN)
    rho_1 = rho_kernel(zeta_rows, cond_other, mine, other, root_rows, "rho_1")
    rho_0x = send(rho_0, CORE)
    rho_1, cond_other, out_00, out_10, rho_0x = lax.optimization_barrier(
        (rho_1, cond_other, out_00, out_10, rho_0x)
    )
    down_1 = send(rho_1, Z_UP)
    up_1 = send(rho_1, Z_DOWN)
    own_01 = slab_kernel(mine, cond_other, zeta_slab, weight[0][1], root_slab, "slab_01")
    rho_1x = send(rho_1, CORE)
    own_01, other, down_0, up_0, rho_1x = lax.optimization_barrier(
        (own_01, other, down_0, up_0, rho_1x)
    )
    far_0 = send(down_0, Z_UP)
    out_01 = send(own_01, Y_PAIR)
    out_11 = send(own_01, Y_CROSS)
    own_10 = slab_kernel(other, cond_mine, zeta_slab, weight[1][0], root_slab, "slab_10")
    own_10, other, down_1, up_1 = lax.optimization_barrier((own_10, other, down_1, up_1))
    far_1 = send(up_1, Z_DOWN)
    own_11 = slab_kernel(other, cond_other, zeta_slab, weight[1][1], root_slab, "slab_11")
    out_side = ([[out_00, out_01], [out_10, out_11]], BF)
    in_side = ([[own_00, own_01], [own_10, own_11]], F32)

    own = [(rho_0, rho_1, False), (rho_0x, rho_1x, True)]
    own_out, own_in = chi_kernel(own, [out_side, in_side], "chi_own")
    got_own = send(own_out, Y_PAIR)
    near = [(down_0, down_1, False), (up_0, up_1, False)]
    near_out, near_in = chi_kernel(near, [out_side, in_side], "chi_near")
    got_near = send(near_out, Y_PAIR)
    own_in, near_in, far_0, far_1, down_0, up_0, down_1, up_1, got_own = lax.optimization_barrier(
        (own_in, near_in, far_0, far_1, down_0, up_0, down_1, up_1, got_own)
    )

    mid = [
        (send(down_0, CORE), send(down_1, CORE), True),
        (send(up_0, CORE), send(up_1, CORE), True),
    ]
    mid_out, mid_in = chi_kernel(mid, [out_side, in_side], "chi_next")
    got_mid = send(mid_out, Y_PAIR)
    far_0x, far_1x = send(far_0, CORE), send(far_1, CORE)
    far_0x, far_1x, mid_in, got_near = lax.optimization_barrier((far_0x, far_1x, mid_in, got_near))
    far = [(far_0, far_1, False), (far_0x, far_1x, True)]
    far_out, far_in = chi_kernel(far, [out_side, in_side], "chi_far")
    got_far = send(far_out, Y_PAIR)

    yl = grow // 8
    z = yz % 4

    def blocks(*pairs):
        return jnp.stack([side * 4 + (z + s) % 4 for side, s in pairs] + [core]).astype(jnp.int32)

    total_rows, cols = chi_prev.shape
    chi = chi_prev.reshape(16, total_rows // 16, cols)
    here, there = yl, 1 - yl
    done = finish_kernel(
        blocks((here, 0), (here, 3), (here, 1), (here, 2), (there, 0), (there, 3), (there, 1)),
        chi,
        [
            (own_in, 0, own_in, 1, 1),
            (near_in, 0, mid_in, 0, 2),
            (far_in, 0, far_in, 1, 1),
            (got_own, 0, got_own, 1, 1),
            (got_near, 0, got_mid, 0, 2),
        ],
        None,
        "finish_most",
    )
    done = finish_kernel(
        blocks((there, 2)), chi, [(got_far, 0, got_far, 1, 1)], done, "finish_far"
    )
    return done.reshape(total_rows, cols)


def solution(mesh):
    placed = (
        P("band", "grow"),
        P(("band", "grow"), None),
        P("grow", None),
        P("band", None, None),
        P(),
        P("grow", None),
        P(),
        P(),
        P(("band", "grow")),
        P("grow"),
    )
    return jax.shard_map(
        on_device, mesh=mesh, in_specs=placed, out_specs=P("band", "grow"), check_vma=False
    )
```
